32 devices in a mesh: dp: 8 (over z, y), section: 4 (over x, core).
Axes of the slice: x: 2, y: 2, z: 4, core: 2. Of those that a mesh axis runs over, the one named last changes fastest.
Arguments:
- held: bfloat16 [4, 1024, 4096], P('section', 'dp'), may hold values from -6 to 6
- norm_gain: bfloat16 [4, 1, 4096], P('section'), may hold values from 0.099609375 to 1.8984375
- w_gate: bfloat16 [4, 1, 4096, 6144], P('section', None, None, 'dp'), may hold values from -0.09375 to 0.09375
- w_up: bfloat16 [4, 1, 4096, 6144], P('section', None, None, 'dp'), may hold values from -0.09375 to 0.09375
- w_down: bfloat16 [4, 1, 6144, 4096], P('section', None, 'dp'), may hold values from -0.078125 to 0.078125
- layer_counts: int32 [4], P('section'), may hold values from 0 to 1, as said below
- query_bank: bfloat16 [128, 4096], P('dp'), may hold values from -0.099609375 to 0.099609375
- pin_bank: bfloat16 [128, 4096], P('dp'), may hold values from -0.099609375 to 0.099609375
- positive: int32 [128], P('dp'), may hold values from 0 to 127, each once
Outputs:
- section_out: bfloat16 [4, 1024, 4096], P('section', 'dp')
- grad_query: float32 [128, 4096], P('dp', 'section')
- grad_pin: float32 [128, 4096], P('dp', 'section')
The draws below stay inside these ranges and needn't reach their ends.
Inputs may be any that keep to these rules, and one draw needn't show every extreme that they name: `layer_counts`: each section's number of applied layer slots; some section applies 1 and some section applies none. Each pin is the positive of exactly one query.
All inputs are finite; a program needn't handle non-finite values.
Results may differ from the reference program's by a relative error of at most 0.012.
Values may be sent and summed in bfloat16 or wider, within the bound.
No kernel may reach another device: no remote copies, remote signals or barrier semaphores. Data moves between devices by JAX's collectives and lax.ppermute only.
A program may use at most 128 MiB of HBM per device.

```python
import jax
import jax.numpy as jnp
from jax import lax

D = 4096
FFW = 6144
SLOTS = 1
LEN = 128
PAIR_DEV = 16
SECTIONS = 4
ROWS = 1024
PAIRS = 128
SPAN = 1
SEQ_MB = 8
N_DP = 8


def draw_layer_counts(key, part):
    key = jax.random.fold_in(key, 7)
    first_key, second_key = jax.random.split(key)
    values = jax.random.randint(first_key, (SECTIONS,), 0, SLOTS + 1)
    order = jax.random.permutation(second_key, SECTIONS)
    values = values.at[order[0]].set(SLOTS)
    values = values.at[order[1]].set(0)
    return values.astype(jnp.int32)


def block_levels(stream_key, extent, pieces, least, high):
    level = 1.0
    for position, blocks in pieces:
        draws = jax.random.uniform(jax.random.fold_in(jax.random.fold_in(stream_key, 6), position), (blocks,), jnp.float32, least / len(pieces), high / len(pieces))
        level = level * jnp.repeat(jnp.exp(draws), extent[position] // blocks).reshape((-1,) + (1,) * (len(extent) - 1 - position))
    return level


def centred(key, extent, scale, limit, shards=(), held_as=jnp.bfloat16):
    loudness = block_levels(key, extent, shards, -0.22, 0.18) if shards else 1.0
    drawn = jax.random.normal(key, extent, jnp.float32) * scale * loudness
    return jnp.minimum(jnp.maximum(drawn, -limit), limit).astype(held_as)


def setup_inputs(seed: int = 0) -> dict:
    splits = jax.random.split(jax.random.key(seed), 10)
    held = centred(splits[0], (SECTIONS, ROWS, D), 1.0, 6.0, ((0, 4), (1, 8)))
    norm_gain = jnp.clip(1.0 + 0.18 * jax.random.normal(splits[1], (SECTIONS, SLOTS, D), jnp.float32), 0.099609375, 1.8984375).astype(jnp.bfloat16)
    w_gate = centred(splits[2], (SECTIONS, SLOTS, D, FFW), D ** -0.5, 0.09375, ((0, 4), (3, 8)))
    w_up = centred(splits[3], (SECTIONS, SLOTS, D, FFW), D ** -0.5, 0.09375, ((0, 4), (3, 8)))
    w_down = centred(splits[4], (SECTIONS, SLOTS, FFW, D), FFW ** -0.5, 0.078125, ((0, 4), (2, 8)))
    layer_counts = draw_layer_counts(jax.random.fold_in(splits[9], 71), 0)
    query_bank = centred(splits[6], (PAIRS, D), 0.015625, 0.099609375, ((0, 8),))
    pin_bank = centred(splits[7], (PAIRS, D), 0.015625, 0.099609375, ((0, 8),))
    positive = jax.random.permutation(splits[8], PAIRS).astype(jnp.int32)
    return {"held": held, "norm_gain": norm_gain, "w_gate": w_gate, "w_up": w_up, "w_down": w_down, "layer_counts": layer_counts, "query_bank": query_bank, "pin_bank": pin_bank, "positive": positive}


INV_TEMP = 20.0
EPSILON = 1e-06

def rms_scaled(stream, gain_row):
    values = stream.astype(jnp.float32)
    factor = lax.rsqrt(lax.optimization_barrier(jnp.mean(values * values, axis=-1, keepdims=True)) + EPSILON)
    return (values * factor * gain_row.astype(jnp.float32)).astype(jnp.bfloat16)

def grouped_down(hidden, down_w):
    shard = FFW // N_DP
    parts = hidden.reshape(hidden.shape[0], N_DP, shard).transpose(1, 0, 2)
    downs = down_w.reshape(N_DP, shard, D)

    def add_group(accum, pair):
        term = jnp.dot(pair[0], pair[1], preferred_element_type=jnp.float32).astype(jnp.bfloat16)
        term = lax.optimization_barrier(term)
        return (accum + term.astype(jnp.float32), None)
    start_sum = jnp.zeros((hidden.shape[0], D), jnp.float32)
    result, _ = lax.scan(add_group, start_sum, (parts, downs))
    return result

def layer_apply(stream, gain_row, gate_w, up_w, down_w):
    normed = rms_scaled(stream, gain_row)
    gate_out = jnp.dot(normed, gate_w, preferred_element_type=jnp.float32)
    up_out = jnp.dot(normed, up_w, preferred_element_type=jnp.float32)
    hidden = (jax.nn.silu(gate_out) * up_out).astype(jnp.bfloat16)
    update = grouped_down(hidden, down_w)
    return (stream.astype(jnp.float32) + update).astype(jnp.bfloat16)

def unit_rows(values):
    floats = values.astype(jnp.float32)
    length = jnp.sqrt(lax.optimization_barrier(jnp.sum(floats * floats, axis=-1, keepdims=True)) + EPSILON)
    return (floats / length, length)

def back_unit(step, unit, length):
    return (step - unit * lax.optimization_barrier(jnp.sum(unit * step, axis=-1, keepdims=True))) / length

def reference(held, norm_gain, w_gate, w_up, w_down, layer_counts, query_bank, pin_bank, positive):
    outputs = []
    for section in range(SECTIONS):
        stream = held[section]
        for slot_index in range(SLOTS):
            moved = layer_apply(stream, norm_gain[section, slot_index], w_gate[section, slot_index], w_up[section, slot_index], w_down[section, slot_index])
            stream = jnp.where(slot_index < layer_counts[section], moved, stream)
        outputs.append(stream)
    section_out = jnp.stack(outputs)
    seq_ids = jnp.arange(SEQ_MB, dtype=jnp.int32)
    fresh_rows = section_out[SECTIONS - 1][((seq_ids + 1) * LEN - 1).astype(jnp.int32)]
    targets = (((seq_ids + 1) * SPAN - 1) * PAIR_DEV).astype(jnp.int32)
    pins = pin_bank.at[targets].set(fresh_rows)
    query_unit, query_length = unit_rows(query_bank)
    pin_unit, pin_length = unit_rows(pins)
    query_send = query_unit.astype(jnp.bfloat16)
    pin_send = pin_unit.astype(jnp.bfloat16)
    scores = lax.dot_general(query_send, pin_send, (((1,), (1,)), ((), ())), preferred_element_type=jnp.float32) * INV_TEMP
    raised = jnp.exp(scores - INV_TEMP)
    probs = raised / lax.optimization_barrier(jnp.sum(raised, axis=1, keepdims=True))
    onehot = (jnp.arange(PAIRS, dtype=jnp.int32)[None, :] == positive[:, None]).astype(jnp.float32)
    weights = ((probs - onehot) * INV_TEMP).astype(jnp.bfloat16)
    query_step = jnp.dot(weights, pin_send, preferred_element_type=jnp.float32)
    pin_step = lax.dot_general(weights, query_send, (((0,), (0,)), ((), ())), preferred_element_type=jnp.float32)
    return (section_out, back_unit(query_step, query_unit, query_length), back_unit(pin_step, pin_unit, pin_length))
```

```python
import functools

import jax
import jax.numpy as jnp
from jax import lax
from jax.experimental import pallas as pl
from jax.experimental.pallas import tpu as pltpu
from jax.sharding import PartitionSpec as P

INV_TEMP = 20.0
EPSILON = 1e-06
BOTH = ("dp", "section")
ANYWHERE = pl.BlockSpec(memory_space=pl.ANY)
IN_VMEM = pl.BlockSpec(memory_space=pltpu.VMEM)


def ring_order(size):
    return list(range(0, size, 2)) + list(range(size - 1, 0, -2))


def rms_scaled(stream, gain_row):
    values = stream.astype(jnp.float32)
    factor = lax.rsqrt(jnp.mean(values * values, axis=-1, keepdims=True) + EPSILON)
    return (values * factor * gain_row.astype(jnp.float32)).astype(jnp.bfloat16)


def unit_rows(values):
    floats = values.astype(jnp.float32)
    length = jnp.sqrt(jnp.sum(floats * floats, axis=-1, keepdims=True) + EPSILON)
    return (floats / length, length)


def add(*values):
    return sum(v.astype(jnp.float32) for v in values).astype(jnp.bfloat16)


def copies_in(pieces, tokens, sems):
    rows = pieces[0].shape[0]
    copies = [
        pltpu.make_async_copy(piece, tokens.at[pl.ds(i * rows, rows)], sems.at[i])
        for i, piece in enumerate(pieces)
    ]
    for copy in copies:
        copy.start()
    return copies


def copies_out(result, outs, sems):
    rows = outs[0].shape[0]
    copies = [
        pltpu.make_async_copy(result.at[pl.ds(i * rows, rows)], out, sems.at[i])
        for i, out in enumerate(outs)
    ]
    for copy in copies:
        copy.start()
    for copy in copies:
        copy.wait()


def gated(tokens, gate, up, hidden):
    gate_out = jnp.dot(tokens[...], gate[...], preferred_element_type=jnp.float32)
    up_out = jnp.dot(tokens[...], up[...], preferred_element_type=jnp.float32)
    hidden[...] = (gate_out / (1 + jnp.exp(-gate_out)) * up_out).astype(jnp.bfloat16)


def lowered(hidden, down, result):
    result[...] = jnp.dot(hidden[...], down[...], preferred_element_type=jnp.float32).astype(
        jnp.bfloat16
    )


def first_kernel(count, *refs):
    pieces, weights, refs = refs[:count], refs[count : count + 3], refs[count + 3 :]
    outs, kept, refs = refs[:count], refs[count : count + 3], refs[count + 3 :]
    tokens, hidden, result, in_sems, out_sems, weight_sems = refs
    loads = copies_in(pieces, tokens, in_sems)
    fetches = [
        pltpu.make_async_copy(weight, keep, weight_sems.at[i])
        for i, (weight, keep) in enumerate(zip(weights, kept))
    ]
    for copy in fetches:
        copy.start()
    for copy in loads + fetches[:2]:
        copy.wait()
    gated(tokens, kept[0], kept[1], hidden)
    fetches[2].wait()
    lowered(hidden, kept[2], result)
    copies_out(result, outs, out_sems)


def next_kernel(count, *refs):
    pieces, weights, refs = refs[:count], refs[count : count + 3], refs[count + 3 :]
    outs, refs = refs[:count], refs[count:]
    tokens, hidden, result, in_sems, out_sems = refs
    for copy in copies_in(pieces, tokens, in_sems):
        copy.wait()
    gated(tokens, weights[0], weights[1], hidden)
    lowered(hidden, weights[2], result)
    copies_out(result, outs, out_sems)


def multiply(pieces, weights, keep):
    count = len(pieces)
    rows, width = pieces[0].shape
    units = weights[0].shape[1]
    scratch = [
        pltpu.VMEM((count * rows, width), jnp.bfloat16),
        pltpu.VMEM((count * rows, units), jnp.bfloat16),
        pltpu.VMEM((count * rows, width), jnp.bfloat16),
        pltpu.SemaphoreType.DMA((count,)),
        pltpu.SemaphoreType.DMA((count,)),
    ]
    out_shape = [jax.ShapeDtypeStruct(p.shape, jnp.bfloat16) for p in pieces]
    params = pltpu.CompilerParams(vmem_limit_bytes=20 << 20)
    cost = pl.CostEstimate(flops=1 << 20, bytes_accessed=1 << 20, transcendentals=0)
    if keep:
        outs = pl.pallas_call(
            functools.partial(first_kernel, count),
            out_shape=out_shape + [pltpu.VMEM(w.shape, w.dtype) for w in weights],
            in_specs=[ANYWHERE] * (count + 3),
            out_specs=[ANYWHERE] * count + [IN_VMEM] * 3,
            scratch_shapes=scratch + [pltpu.SemaphoreType.DMA((3,))],
            compiler_params=params,
            cost_estimate=cost,
        )(*pieces, *weights)
        return tuple(outs[:count]), outs[count:]
    weights = [pltpu.with_memory_space_constraint(w, pltpu.VMEM) for w in weights]
    return pl.pallas_call(
        functools.partial(next_kernel, count),
        out_shape=out_shape,
        in_specs=[ANYWHERE] * count + [IN_VMEM] * 3,
        out_specs=[ANYWHERE] * count,
        scratch_shapes=scratch,
        compiler_params=params,
        cost_estimate=cost,
    )(*pieces, *weights)


def local(held, norm_gain, w_gate, w_up, w_down, layer_counts, query_bank, pin_bank, positive):
    replicas = lax.axis_size("dp")
    sections = lax.axis_size("section")
    rows_dev, model_width = held.shape[1:]
    pair_dev = query_bank.shape[0]
    half = replicas // 2
    cut = rows_dev // 2
    order = ring_order(replicas)
    place = [order.index(replica) for replica in range(replicas)]
    ring = [(order[i], order[(i + 1) % replicas]) for i in range(replicas)]
    ring_back = [(b, a) for a, b in ring]
    me = lax.axis_index("dp")
    section = lax.axis_index("section")
    position = jnp.array(place, jnp.int32)[me]
    last = sections - 1
    active = layer_counts[0] > 0
    stream = held[0]
    col_width = model_width // sections
    col_start = section * col_width

    def forward(values):
        return lax.ppermute(values, "dp", ring)

    def backward(values):
        return lax.ppermute(values, "dp", ring_back)

    def own_columns(values):
        return lax.dynamic_slice_in_dim(values, col_start, col_width, 1)

    def gathered(values):
        reach = 1
        while reach < replicas:
            other = lax.ppermute(values, "dp", [(i, i ^ reach) for i in range(replicas)])
            lower = (me & reach) == 0
            values = jnp.concatenate(
                [jnp.where(lower, values, other), jnp.where(lower, other, values)], axis=1
            )
            reach *= 2
        return values

    def added_up(values):
        reach = 1
        while reach < replicas:
            pairs = [(i * sections + last, (i ^ reach) * sections + last) for i in range(replicas)]
            values = values + lax.ppermute(values, BOTH, pairs)
            reach *= 2
        return values

    def with_held(rows):
        rows = jnp.concatenate([rows, rows]).astype(jnp.float32)
        rows = lax.dynamic_slice_in_dim(rows, replicas - position, replicas, 0)
        mine = jnp.arange(replicas)[:, None] == position
        return rows + jnp.where(mine, stream[rows_dev - 1 :].astype(jnp.float32), 0.0)

    query_unit, query_length = unit_rows(query_bank)
    query_send = query_unit.astype(jnp.bfloat16)
    pin_unit, pin_length = unit_rows(pin_bank)
    pin_send = pin_unit.astype(jnp.bfloat16)
    own_targets = jnp.zeros((pair_dev, col_width), jnp.bfloat16)
    own_targets = own_targets.at[:, 0].set(positive.astype(jnp.bfloat16))
    own_sends = jnp.stack([own_columns(query_send), own_columns(pin_send), own_targets])

    def gather_and_multiply(own_sends):
        normed = rms_scaled(stream, norm_gain[0])
        f_top, f_low = normed[:cut], normed[cut:]
        b_top, b_low = f_top, f_low
        f_top, b_low = forward(f_top), backward(b_low)
        f_low, b_top = forward(f_low), backward(b_top)
        own, weights = multiply(
            [normed[:cut], normed[cut:]], [w_gate[0, 0], w_up[0, 0], w_down[0, 0]], True
        )
        terms_f, terms_b = [], []
        for step in range(1, half):
            arrived = [f_top, f_low, b_top, b_low]
            f_top, b_low = forward(f_top), backward(b_low)
            if step < half - 1:
                f_low, b_top = forward(f_low), backward(b_top)
            terms = multiply(arrived, weights, False)
            terms_f.append(terms[:2])
            terms_b.append(terms[2:])
        f_low, b_top = forward(terms_b[-1][1]), backward(terms_f[-1][0])
        far = multiply([f_top, b_low], weights, False)
        f_top, b_low = forward(far[0]), backward(far[1])
        in_order = [own] + terms_b + [far] + terms_f[::-1]
        rows = jnp.concatenate([t[1][cut - 1 :] for t in in_order])
        fresh = added_up(with_held(rows)).astype(jnp.bfloat16)
        sends = gathered(own_sends)
        return own, tuple(terms_f), tuple(terms_b), (f_top, f_low, b_top, b_low), fresh, sends

    def gather_only(own_sends):
        fresh = added_up(with_held(jnp.zeros((replicas, model_width), jnp.float32)))
        empty = jnp.zeros((cut, model_width), jnp.bfloat16)
        some = tuple((empty, empty) for _ in range(1, half))
        return (
            (empty, empty),
            some,
            some,
            (empty,) * 4,
            fresh.astype(jnp.bfloat16),
            gathered(own_sends),
        )

    own, terms_f, terms_b, moving, fresh, sends = lax.cond(
        active, gather_and_multiply, gather_only, own_sends
    )

    targets = sends[2, :, 0].astype(jnp.int32)
    pairs = sends.shape[1]
    message = jnp.concatenate(
        [sends[0], sends[1], fresh.reshape(replicas * sections, col_width)]
    )
    messages = [message] + [
        lax.ppermute(message, "section", [(s, (s - step) % sections) for s in range(sections)])
        for step in range(1, sections)
    ]

    def reduce_middle(moving):
        f_top, f_low, b_top, b_low = moving
        for distance in range(half - 1, 1, -1):
            to_f, to_b = terms_b[distance - 1], terms_f[distance - 1]
            if distance < half - 1:
                f_low, b_top = forward(add(to_f[1], f_low)), backward(add(to_b[0], b_top))
            f_top, b_low = forward(add(to_f[0], f_top)), backward(add(to_b[1], b_low))
        return f_top, f_low, b_top, b_low

    moving = lax.cond(active, reduce_middle, lambda moving: moving, moving)

    def loss(messages):
        fresh_rows = sum(
            jnp.where(section == (last - step) % sections, message[2 * pairs :], 0)
            for step, message in enumerate(messages)
        ).reshape(replicas, model_width)
        fresh_rows = jnp.stack([fresh_rows[place[replica]] for replica in range(replicas)])
        fresh_unit, fresh_length = unit_rows(fresh_rows)
        fresh_send = fresh_unit.astype(jnp.bfloat16)
        turned = lax.dynamic_slice_in_dim(
            jnp.concatenate([fresh_send, fresh_send], axis=1), col_start, model_width, 1
        )
        queries = jnp.concatenate([m[:pairs] for m in messages], axis=1)
        pins = jnp.concatenate([m[pairs : 2 * pairs] for m in messages], axis=1)
        pins = pins.reshape(replicas, pair_dev, model_width)
        pins = jnp.concatenate([turned[:, None], pins[:, 1:]], axis=1).reshape(-1, model_width)
        cosines = lax.dot_general(
            queries, pins, (((1,), (1,)), ((), ())), preferred_element_type=jnp.float32
        )
        raised = jnp.exp(INV_TEMP * cosines - INV_TEMP)
        probs = raised / jnp.sum(raised, axis=1, keepdims=True)
        columns = jnp.arange(pairs, dtype=jnp.int32)
        onehot = (columns[None, :] == targets[:, None]).astype(jnp.float32)
        weights = ((probs - onehot) * INV_TEMP).astype(jnp.bfloat16)
        row_start = me * pair_dev
        dots = weights.astype(jnp.float32) * cosines
        query_weights = lax.dynamic_slice_in_dim(weights, row_start, pair_dev, 0)
        pin_weights = lax.dynamic_slice_in_dim(weights, row_start, pair_dev, 1)
        query_dot = lax.dynamic_slice_in_dim(jnp.sum(dots, axis=1), row_start, pair_dev, 0)
        pin_dot = lax.dynamic_slice_in_dim(jnp.sum(dots, axis=0), row_start, pair_dev, 0)
        query_step = jnp.dot(
            query_weights, pins[:, :col_width], preferred_element_type=jnp.float32
        )
        pin_step = lax.dot_general(
            pin_weights,
            queries[:, :col_width],
            (((0,), (0,)), ((), ())),
            preferred_element_type=jnp.float32,
        )
        own_unit = lax.dynamic_slice_in_dim(fresh_unit, me, 1, 0)
        own_length = lax.dynamic_slice_in_dim(fresh_length, me, 1, 0)
        own_unit = jnp.concatenate([own_columns(own_unit), own_columns(pin_unit)[1:]])
        own_length = jnp.concatenate([own_length, pin_length[1:]])
        grad_query = (query_step - own_columns(query_unit) * query_dot[:, None]) / query_length
        grad_pin = (pin_step - own_unit * pin_dot[:, None]) / own_length
        return grad_query, grad_pin

    def reduce_last(moving, messages):
        f_top, f_low, b_top, b_low = moving
        to_f, to_b = terms_b[0], terms_f[0]
        f_low, b_top = forward(add(to_f[1], f_low)), backward(add(to_b[0], b_top))
        f_top, b_low = forward(add(to_f[0], f_top)), backward(add(to_b[1], b_low))
        grads = loss(messages)
        top = add(stream[:cut], own[0], f_top, b_top)
        low = add(stream[cut:], own[1], f_low, b_low)
        return jnp.concatenate([top, low]), *grads

    def keep_stream(moving, messages):
        return stream, *loss(messages)

    stream, grad_query, grad_pin = lax.cond(active, reduce_last, keep_stream, moving, messages)
    return (stream[None], grad_query, grad_pin)


def solution(mesh):
    return jax.shard_map(
        local,
        mesh=mesh,
        in_specs=(
            P("section", "dp", None),
            P("section", None, None),
            P("section", None, None, "dp"),
            P("section", None, None, "dp"),
            P("section", None, "dp", None),
            P("section"),
            P("dp", None),
            P("dp", None),
            P("dp"),
        ),
        out_specs=(P("section", "dp", None), P("dp", "section"), P("dp", "section")),
        check_vma=False,
    )
```

```python
import functools

import jax
import jax.numpy as jnp
from jax import lax
from jax.experimental import pallas as pl
from jax.experimental.pallas import tpu as pltpu
from jax.sharding import PartitionSpec as P

INV_TEMP = 20.0
EPSILON = 1e-06
BOTH = ("dp", "section")
ANYWHERE = pl.BlockSpec(memory_space=pl.ANY)
IN_VMEM = pl.BlockSpec(memory_space=pltpu.VMEM)


def ring_order(size):
    return list(range(0, size, 2)) + list(range(size - 1, 0, -2))


def rms_scaled(stream, gain_row):
    values = stream.astype(jnp.float32)
    factor = lax.rsqrt(jnp.mean(values * values, axis=-1, keepdims=True) + EPSILON)
    return (values * factor * gain_row.astype(jnp.float32)).astype(jnp.bfloat16)


def unit_rows(values):
    floats = values.astype(jnp.float32)
    length = jnp.sqrt(jnp.sum(floats * floats, axis=-1, keepdims=True) + EPSILON)
    return (floats / length, length)


def copies_in(pieces, tokens, sems):
    rows = pieces[0].shape[0]
    copies = [
        pltpu.make_async_copy(piece, tokens.at[pl.ds(i * rows, rows)], sems.at[i])
        for i, piece in enumerate(pieces)
    ]
    for copy in copies:
        copy.start()
    return copies


def copies_out(result, outs, sems):
    rows = outs[0].shape[0]
    copies = [
        pltpu.make_async_copy(result.at[pl.ds(i * rows, rows)], out, sems.at[i])
        for i, out in enumerate(outs)
    ]
    for copy in copies:
        copy.start()
    for copy in copies:
        copy.wait()


def gated(tokens, gate, up, hidden):
    gate_out = jnp.dot(tokens[...], gate[...], preferred_element_type=jnp.float32)
    up_out = jnp.dot(tokens[...], up[...], preferred_element_type=jnp.float32)
    hidden[...] = (gate_out / (1 + jnp.exp(-gate_out)) * up_out).astype(jnp.bfloat16)


def lowered(hidden, down, result):
    result[...] = jnp.dot(hidden[...], down[...], preferred_element_type=jnp.float32).astype(
        jnp.bfloat16
    )


def first_kernel(count, *refs):
    pieces, weights, refs = refs[:count], refs[count : count + 3], refs[count + 3 :]
    outs, kept, refs = refs[:count], refs[count : count + 3], refs[count + 3 :]
    tokens, hidden, result, in_sems, out_sems, weight_sems = refs
    loads = copies_in(pieces, tokens, in_sems)
    fetches = [
        pltpu.make_async_copy(weight, keep, weight_sems.at[i])
        for i, (weight, keep) in enumerate(zip(weights, kept))
    ]
    for copy in fetches:
        copy.start()
    for copy in loads + fetches[:2]:
        copy.wait()
    gated(tokens, kept[0], kept[1], hidden)
    fetches[2].wait()
    lowered(hidden, kept[2], result)
    copies_out(result, outs, out_sems)


def next_kernel(count, *refs):
    pieces, weights, refs = refs[:count], refs[count : count + 3], refs[count + 3 :]
    outs, refs = refs[:count], refs[count:]
    tokens, hidden, result, in_sems, out_sems = refs
    for copy in copies_in(pieces, tokens, in_sems):
        copy.wait()
    gated(tokens, weights[0], weights[1], hidden)
    lowered(hidden, weights[2], result)
    copies_out(result, outs, out_sems)


def multiply(pieces, weights, keep):
    count = len(pieces)
    rows, width = pieces[0].shape
    units = weights[0].shape[1]
    scratch = [
        pltpu.VMEM((count * rows, width), jnp.bfloat16),
        pltpu.VMEM((count * rows, units), jnp.bfloat16),
        pltpu.VMEM((count * rows, width), jnp.bfloat16),
        pltpu.SemaphoreType.DMA((count,)),
        pltpu.SemaphoreType.DMA((count,)),
    ]
    out_shape = [jax.ShapeDtypeStruct(p.shape, jnp.bfloat16) for p in pieces]
    params = pltpu.CompilerParams(vmem_limit_bytes=20 << 20)
    tokens = count * rows
    cost = pl.CostEstimate(
        flops=6 * tokens * width * units, bytes_accessed=4 * tokens * width, transcendentals=0
    )
    if keep:
        outs = pl.pallas_call(
            functools.partial(first_kernel, count),
            out_shape=out_shape + [pltpu.VMEM(w.shape, w.dtype) for w in weights],
            in_specs=[ANYWHERE] * (count + 3),
            out_specs=[ANYWHERE] * count + [IN_VMEM] * 3,
            scratch_shapes=scratch + [pltpu.SemaphoreType.DMA((3,))],
            compiler_params=params,
            cost_estimate=cost,
        )(*pieces, *weights)
        return tuple(outs[:count]), outs[count:]
    weights = [pltpu.with_memory_space_constraint(w, pltpu.VMEM) for w in weights]
    return pl.pallas_call(
        functools.partial(next_kernel, count),
        out_shape=out_shape,
        in_specs=[ANYWHERE] * count + [IN_VMEM] * 3,
        out_specs=[ANYWHERE] * count,
        scratch_shapes=scratch,
        compiler_params=params,
        cost_estimate=cost,
    )(*pieces, *weights)


def sum_kernel(plan, sources, *refs):
    ins, outs, (loaded, result, in_sems, out_sems) = refs[:sources], refs[sources:-4], refs[-4:]
    rows = result.shape[1]
    part = rows // 2
    groups, slot = [], 0
    for group, (terms, out, out_row) in enumerate(plan):
        for cut in range(2):
            copies = []
            for i, (source, row) in enumerate(terms):
                copies.append(
                    pltpu.make_async_copy(
                        ins[source].at[pl.ds(row + cut * part, part)],
                        loaded.at[slot + i, pl.ds(cut * part, part)],
                        in_sems.at[2 * (slot + i) + cut],
                    )
                )
            groups.append((group, cut, slot, copies, out, out_row))
        slot += len(terms)
    for entry in groups:
        for copy in entry[3]:
            copy.start()
    stores = []
    for group, cut, slot, copies, out, out_row in groups:
        for copy in copies:
            copy.wait()
        here = slice(cut * part, (cut + 1) * part)
        total = loaded[slot, here].astype(jnp.float32)
        for i in range(1, len(copies)):
            total = total + loaded[slot + i, here].astype(jnp.float32)
        result[group, here] = total.astype(jnp.bfloat16)
        store = pltpu.make_async_copy(
            result.at[group, pl.ds(cut * part, part)],
            outs[out].at[pl.ds(out_row + cut * part, part)],
            out_sems.at[2 * group + cut],
        )
        store.start()
        stores.append(store)
    for store in stores:
        store.wait()


def sums(plan, sources, rows, out_shapes):
    terms = sum(len(entry[0]) for entry in plan)
    width = sources[0].shape[1]
    return pl.pallas_call(
        functools.partial(sum_kernel, plan, len(sources)),
        out_shape=[jax.ShapeDtypeStruct(shape, jnp.bfloat16) for shape in out_shapes],
        in_specs=[ANYWHERE] * len(sources),
        out_specs=[ANYWHERE] * len(out_shapes),
        scratch_shapes=[
            pltpu.VMEM((terms, rows, width), jnp.bfloat16),
            pltpu.VMEM((len(plan), rows, width), jnp.bfloat16),
            pltpu.SemaphoreType.DMA((2 * terms,)),
            pltpu.SemaphoreType.DMA((2 * len(plan),)),
        ],
        compiler_params=pltpu.CompilerParams(vmem_limit_bytes=16 << 20),
        cost_estimate=pl.CostEstimate(
            flops=terms * rows * width, bytes_accessed=4 * terms * rows * width, transcendentals=0
        ),
    )(*sources)


def two_sums(first, second):
    shape = first[0].shape
    plan = (((((0, 0), (1, 0))), 0, 0), ((((2, 0), (3, 0))), 1, 0))
    return sums(plan, [*first, *second], shape[0], [shape, shape])


def local(held, norm_gain, w_gate, w_up, w_down, layer_counts, query_bank, pin_bank, positive):
    replicas = lax.axis_size("dp")
    sections = lax.axis_size("section")
    rows_dev, model_width = held.shape[1:]
    pair_dev = query_bank.shape[0]
    half = replicas // 2
    cut = rows_dev // 2
    order = ring_order(replicas)
    place = [order.index(replica) for replica in range(replicas)]
    ring = [(order[i], order[(i + 1) % replicas]) for i in range(replicas)]
    ring_back = [(b, a) for a, b in ring]
    me = lax.axis_index("dp")
    section = lax.axis_index("section")
    position = jnp.array(place, jnp.int32)[me]
    turn = (replicas - position).astype(jnp.uint32)
    mine = jnp.arange(replicas)[:, None] == position
    last = sections - 1
    active = layer_counts[0] > 0
    stream = held[0]
    col_width = model_width // sections
    col_start = (section * col_width).astype(jnp.uint32)
    turn, mine, col_start = lax.optimization_barrier((turn, mine, col_start))

    def forward(values):
        return lax.ppermute(values, "dp", ring)

    def backward(values):
        return lax.ppermute(values, "dp", ring_back)

    def own_columns(values):
        return lax.dynamic_slice(values, (jnp.uint32(0), col_start), (values.shape[0], col_width))

    def after(values, others):
        return lax.optimization_barrier((values, others))[0]

    def doubled(values, reach):
        other = lax.ppermute(values, "dp", [(i, i ^ reach) for i in range(replicas)])
        return jnp.concatenate([values, other], axis=1)

    def gathered(values, reach):
        while reach < replicas:
            values = doubled(values, reach)
            reach *= 2
        return values

    def added_up(values):
        reach = 1
        while reach < replicas:
            pairs = [(i * sections + last, (i ^ reach) * sections + last) for i in range(replicas)]
            values = values + lax.ppermute(values, BOTH, pairs)
            reach *= 2
        return values

    def with_held(rows):
        rows = jnp.concatenate([rows, rows]).astype(jnp.float32)
        rows = lax.dynamic_slice(rows, (turn, jnp.uint32(0)), (replicas, model_width))
        return rows + jnp.where(mine, stream[rows_dev - 1 :].astype(jnp.float32), 0.0)

    def unit_columns():
        query_send = unit_rows(query_bank)[0].astype(jnp.bfloat16)
        pin_send = unit_rows(pin_bank)[0].astype(jnp.bfloat16)
        targets = jnp.broadcast_to(positive.astype(jnp.bfloat16)[:, None], (pair_dev, col_width))
        return jnp.stack([own_columns(query_send), own_columns(pin_send), targets])

    def gather_and_multiply():
        normed = rms_scaled(stream, norm_gain[0])
        f_top, f_low = normed[:cut], normed[cut:]
        b_top, b_low = f_top, f_low
        f_top, b_low = forward(f_top), backward(b_low)
        f_low, b_top = forward(f_low), backward(b_top)
        own, weights = multiply(
            [normed[:cut], normed[cut:]], [w_gate[0, 0], w_up[0, 0], w_down[0, 0]], True
        )
        sends = doubled(unit_columns(), 1)
        reach = 2
        ready = (own, sends)
        terms_f, terms_b = [], []
        for step in range(1, half):
            arrived = [f_top, f_low, b_top, b_low]
            f_top, f_low, b_top, b_low = after(arrived, ready)
            f_top, b_low = forward(f_top), backward(b_low)
            if step < half - 1:
                f_low, b_top = forward(f_low), backward(b_top)
            if reach < replicas:
                sends = doubled(after(sends, arrived), reach)
                reach *= 2
            terms = multiply(arrived, weights, False)
            terms_f.append(terms[:2])
            terms_b.append(terms[2:])
            ready = (terms, sends)
        sends = gathered(sends, reach)
        f_low, b_top = forward(terms_b[-1][1]), backward(terms_f[-1][0])
        far = multiply([f_top, b_low], weights, False)
        f_top, b_low = forward(far[0]), backward(far[1])
        in_order = [own] + terms_b + [far] + terms_f[::-1]
        rows = jnp.concatenate([t[1][cut - 1 :] for t in in_order])
        fresh = added_up(with_held(rows)).astype(jnp.bfloat16)
        return own, tuple(terms_f), tuple(terms_b), (f_top, f_low, b_top, b_low), fresh, sends

    def gather_only():
        fresh = added_up(with_held(jnp.zeros((replicas, model_width), jnp.float32)))
        empty = jnp.zeros((cut, model_width), jnp.bfloat16)
        some = tuple((empty, empty) for _ in range(1, half))
        return (
            (empty, empty),
            some,
            some,
            (empty,) * 4,
            fresh.astype(jnp.bfloat16),
            gathered(unit_columns(), 1),
        )

    own, terms_f, terms_b, moving, fresh, sends = lax.cond(
        active, gather_and_multiply, gather_only
    )

    pairs = sends.shape[1]
    fresh = jnp.stack([fresh[place[replica]] for replica in range(replicas)])
    fresh = jnp.where(section == last, fresh, jnp.zeros_like(fresh))
    fresh = fresh.reshape(replicas * sections, col_width)
    units = sends[:2].reshape(2 * pairs, col_width)

    def section_swap(units, fresh, reach):
        message = jnp.concatenate([units, fresh])
        other = lax.ppermute(message, "section", [(s, s ^ reach) for s in range(sections)])
        return other[: units.shape[0]], fresh + other[units.shape[0] :]

    offsets = [0, sections // 2]
    swapped = section_swap(units, fresh, sections // 2)

    def reduce_middle(moving):
        f_top, f_low, b_top, b_low = moving
        for distance in range(half - 1, 1, -1):
            to_f, to_b = terms_b[distance - 1], terms_f[distance - 1]
            if distance < half - 1:
                f_low, b_top = two_sums((to_f[1], f_low), (to_b[0], b_top))
                f_low, b_top = forward(f_low), backward(b_top)
            f_top, b_low = two_sums((to_f[0], f_top), (to_b[1], b_low))
            f_top, b_low = forward(f_top), backward(b_low)
        return f_top, f_low, b_top, b_low

    moving = lax.cond(active, reduce_middle, lambda moving: moving, moving)
    swapped, moving = lax.optimization_barrier((swapped, moving))
    units, fresh = [units, swapped[0]], swapped[1]
    reach = sections // 4
    while reach:
        other, fresh = section_swap(jnp.concatenate(units), fresh, reach)
        units += list(other.reshape(len(units), 2 * pairs, col_width))
        offsets += [offset ^ reach for offset in offsets]
        reach //= 2
    offsets = jnp.array(offsets, jnp.int32)

    def loss(units, fresh):
        wanted = (me ^ jnp.arange(replicas))[:, None] * sections + (section ^ offsets)[None, :]
        pick = wanted.reshape(-1, 1) == jnp.arange(replicas * sections)[None, :]
        fresh_rows = jnp.dot(pick.astype(jnp.bfloat16), fresh, preferred_element_type=jnp.float32)
        fresh_rows = fresh_rows.reshape(replicas, sections, col_width)
        fresh_length = jnp.sqrt(
            jnp.sum(fresh_rows * fresh_rows, axis=(1, 2), keepdims=True) + EPSILON
        )
        fresh_unit = fresh_rows / fresh_length
        fresh_send = fresh_unit.astype(jnp.bfloat16)
        is_fresh = (jnp.arange(pair_dev) == 0)[None, :, None]
        queries = [u[:pairs] for u in units]
        pins = [
            jnp.where(
                is_fresh,
                fresh_send[:, i : i + 1],
                u[pairs:].reshape(replicas, pair_dev, col_width),
            ).reshape(pairs, col_width)
            for i, u in enumerate(units)
        ]
        cosines = sum(
            lax.dot_general(q, p, (((1,), (1,)), ((), ())), preferred_element_type=jnp.float32)
            for q, p in zip(queries, pins)
        )
        raised = jnp.exp(INV_TEMP * cosines - INV_TEMP)
        probs = raised / jnp.sum(raised, axis=1, keepdims=True)
        numbers = (me ^ jnp.arange(replicas))[:, None] * pair_dev + jnp.arange(pair_dev)[None, :]
        targets = sends[2, :, 0].astype(jnp.int32)
        onehot = (numbers.reshape(1, -1) == targets[:, None]).astype(jnp.float32)
        weights = ((probs - onehot) * INV_TEMP).astype(jnp.bfloat16)
        dots = weights.astype(jnp.float32) * cosines
        query_dot = jnp.sum(dots[:pair_dev], axis=1)
        pin_dot = jnp.sum(dots[:, :pair_dev], axis=0)
        query_step = jnp.dot(weights[:pair_dev], pins[0], preferred_element_type=jnp.float32)
        pin_step = lax.dot_general(
            weights[:, :pair_dev],
            queries[0],
            (((0,), (0,)), ((), ())),
            preferred_element_type=jnp.float32,
        )
        query_unit, query_length = unit_rows(query_bank)
        pin_unit, pin_length = unit_rows(pin_bank)
        own_unit = jnp.concatenate([fresh_unit[0, :1], own_columns(pin_unit)[1:]])
        own_length = jnp.concatenate([fresh_length[0], pin_length[1:]])
        grad_query = (query_step - own_columns(query_unit) * query_dot[:, None]) / query_length
        grad_pin = (pin_step - own_unit * pin_dot[:, None]) / own_length
        return grad_query, grad_pin

    def reduce_last(moving, units, fresh):
        f_top, f_low, b_top, b_low = moving
        to_f, to_b = terms_b[0], terms_f[0]
        f_low, b_top = two_sums((to_f[1], f_low), (to_b[0], b_top))
        f_low, b_top = forward(f_low), backward(b_top)
        f_top, b_low = two_sums((to_f[0], f_top), (to_b[1], b_low))
        f_top, b_low = forward(f_top), backward(b_low)
        grads = loss(units, fresh)
        plan = (
            (((0, 0), (1, 0), (3, 0), (5, 0)), 0, 0),
            (((0, cut), (2, 0), (4, 0), (6, 0)), 0, cut),
        )
        sources = [stream, *own, f_top, f_low, b_top, b_low]
        return *sums(plan, sources, cut, [stream.shape]), *grads

    def keep_stream(moving, units, fresh):
        return stream + jnp.concatenate(own), *loss(units, fresh)

    stream_out, grad_query, grad_pin = lax.cond(active, reduce_last, keep_stream, moving, units, fresh)
    return (stream_out[None], grad_query, grad_pin)


def solution(mesh):
    return jax.shard_map(
        local,
        mesh=mesh,
        in_specs=(
            P("section", "dp", None),
            P("section", None, None),
            P("section", None, None, "dp"),
            P("section", None, None, "dp"),
            P("section", None, "dp", None),
            P("section"),
            P("dp", None),
            P("dp", None),
            P("dp"),
        ),
        out_specs=(P("section", "dp", None), P("dp", "section"), P("dp", "section")),
        check_vma=False,
    )
```

```python
import functools

import jax
import jax.numpy as jnp
from jax import lax
from jax.experimental import pallas as pl
from jax.experimental.pallas import tpu as pltpu
from jax.sharding import PartitionSpec as P

INV_TEMP = 20.0
EPSILON = 1e-06
BOTH = ("dp", "section")
ANYWHERE = pl.BlockSpec(memory_space=pl.ANY)
IN_VMEM = pl.BlockSpec(memory_space=pltpu.VMEM)


def ring_order(size):
    return list(range(0, size, 2)) + list(range(size - 1, 0, -2))


def rms_scaled(stream, gain_row):
    values = stream.astype(jnp.float32)
    factor = lax.rsqrt(jnp.mean(values * values, axis=-1, keepdims=True) + EPSILON)
    return (values * factor * gain_row.astype(jnp.float32)).astype(jnp.bfloat16)


def unit_rows(values):
    floats = values.astype(jnp.float32)
    length = jnp.sqrt(jnp.sum(floats * floats, axis=-1, keepdims=True) + EPSILON)
    return (floats / length, length)


def copies_in(pieces, tokens, sems):
    rows = pieces[0].shape[0]
    copies = [
        pltpu.make_async_copy(piece, tokens.at[pl.ds(i * rows, rows)], sems.at[i])
        for i, piece in enumerate(pieces)
    ]
    for copy in copies:
        copy.start()
    return copies


def copies_out(result, outs, sems):
    rows = outs[0].shape[0]
    copies = [
        pltpu.make_async_copy(result.at[pl.ds(i * rows, rows)], out, sems.at[i])
        for i, out in enumerate(outs)
    ]
    for copy in copies:
        copy.start()
    for copy in copies:
        copy.wait()


def gated(tokens, gate, up, hidden):
    gate_out = jnp.dot(tokens[...], gate[...], preferred_element_type=jnp.float32)
    up_out = jnp.dot(tokens[...], up[...], preferred_element_type=jnp.float32)
    hidden[...] = (gate_out / (1 + jnp.exp(-gate_out)) * up_out).astype(jnp.bfloat16)


def lowered(hidden, down, result):
    result[...] = jnp.dot(hidden[...], down[...], preferred_element_type=jnp.float32).astype(
        jnp.bfloat16
    )


def last_rows(result, count, tails):
    rows = result.shape[0] // count
    for i in range(count):
        end = result[(i + 1) * rows - 16 : (i + 1) * rows].astype(jnp.float32)
        tails[i : i + 1] = end[15:]


def first_kernel(count, *refs):
    pieces, weights, refs = refs[:count], refs[count : count + 3], refs[count + 3 :]
    outs, tails, kept, refs = refs[:count], refs[count], refs[count + 1 : count + 4], refs[count + 4 :]
    tokens, hidden, result, in_sems, out_sems, weight_sems = refs
    loads = copies_in(pieces, tokens, in_sems)
    fetches = [
        pltpu.make_async_copy(weight, keep, weight_sems.at[i])
        for i, (weight, keep) in enumerate(zip(weights, kept))
    ]
    for copy in fetches:
        copy.start()
    for copy in loads + fetches[:2]:
        copy.wait()
    gated(tokens, kept[0], kept[1], hidden)
    fetches[2].wait()
    lowered(hidden, kept[2], result)
    last_rows(result, count, tails)
    copies_out(result, outs, out_sems)


def next_kernel(count, *refs):
    pieces, weights, refs = refs[:count], refs[count : count + 3], refs[count + 3 :]
    outs, tails, refs = refs[:count], refs[count], refs[count + 1 :]
    tokens, hidden, result, in_sems, out_sems = refs
    for copy in copies_in(pieces, tokens, in_sems):
        copy.wait()
    gated(tokens, weights[0], weights[1], hidden)
    lowered(hidden, weights[2], result)
    last_rows(result, count, tails)
    copies_out(result, outs, out_sems)


def multiply(pieces, weights, keep):
    count = len(pieces)
    rows, width = pieces[0].shape
    units = weights[0].shape[1]
    scratch = [
        pltpu.VMEM((count * rows, width), jnp.bfloat16),
        pltpu.VMEM((count * rows, units), jnp.bfloat16),
        pltpu.VMEM((count * rows, width), jnp.bfloat16),
        pltpu.SemaphoreType.DMA((count,)),
        pltpu.SemaphoreType.DMA((count,)),
    ]
    out_shape = [jax.ShapeDtypeStruct(p.shape, jnp.bfloat16) for p in pieces]
    out_shape += [jax.ShapeDtypeStruct((8, width), jnp.float32)]
    params = pltpu.CompilerParams(vmem_limit_bytes=20 << 20)
    tokens = count * rows
    cost = pl.CostEstimate(
        flops=6 * tokens * width * units, bytes_accessed=4 * tokens * width, transcendentals=0
    )
    if keep:
        outs = pl.pallas_call(
            functools.partial(first_kernel, count),
            out_shape=out_shape + [pltpu.VMEM(w.shape, w.dtype) for w in weights],
            in_specs=[ANYWHERE] * (count + 3),
            out_specs=[ANYWHERE] * count + [IN_VMEM] * 4,
            scratch_shapes=scratch + [pltpu.SemaphoreType.DMA((3,))],
            compiler_params=params,
            cost_estimate=cost,
        )(*pieces, *weights)
        return outs[:count], outs[count], outs[count + 1 :]
    weights = [pltpu.with_memory_space_constraint(w, pltpu.VMEM) for w in weights]
    outs = pl.pallas_call(
        functools.partial(next_kernel, count),
        out_shape=out_shape,
        in_specs=[ANYWHERE] * count + [IN_VMEM] * 3,
        out_specs=[ANYWHERE] * count + [IN_VMEM],
        scratch_shapes=scratch,
        compiler_params=params,
        cost_estimate=cost,
    )(*pieces, *weights)
    return outs[:count], outs[count]


def sum_kernel(plan, sources, *refs):
    ins, outs, (loaded, result, in_sems, out_sems) = refs[:sources], refs[sources:-4], refs[-4:]
    rows = result.shape[1]
    part = rows // 2
    groups, slot = [], 0
    for group, (terms, out, out_row) in enumerate(plan):
        for cut in range(2):
            copies = []
            for i, (source, row) in enumerate(terms):
                copies.append(
                    pltpu.make_async_copy(
                        ins[source].at[pl.ds(row + cut * part, part)],
                        loaded.at[slot + i, pl.ds(cut * part, part)],
                        in_sems.at[2 * (slot + i) + cut],
                    )
                )
            groups.append((group, cut, slot, copies, out, out_row))
        slot += len(terms)
    for entry in groups:
        for copy in entry[3]:
            copy.start()
    stores = []
    for group, cut, slot, copies, out, out_row in groups:
        for copy in copies:
            copy.wait()
        here = slice(cut * part, (cut + 1) * part)
        total = loaded[slot, here].astype(jnp.float32)
        for i in range(1, len(copies)):
            total = total + loaded[slot + i, here].astype(jnp.float32)
        result[group, here] = total.astype(jnp.bfloat16)
        store = pltpu.make_async_copy(
            result.at[group, pl.ds(cut * part, part)],
            outs[out].at[pl.ds(out_row + cut * part, part)],
            out_sems.at[2 * group + cut],
        )
        store.start()
        stores.append(store)
    for store in stores:
        store.wait()


def sums(plan, sources, rows, out_shapes):
    terms = sum(len(entry[0]) for entry in plan)
    width = sources[0].shape[1]
    return pl.pallas_call(
        functools.partial(sum_kernel, plan, len(sources)),
        out_shape=[jax.ShapeDtypeStruct(shape, jnp.bfloat16) for shape in out_shapes],
        in_specs=[ANYWHERE] * len(sources),
        out_specs=[ANYWHERE] * len(out_shapes),
        scratch_shapes=[
            pltpu.VMEM((terms, rows, width), jnp.bfloat16),
            pltpu.VMEM((len(plan), rows, width), jnp.bfloat16),
            pltpu.SemaphoreType.DMA((2 * terms,)),
            pltpu.SemaphoreType.DMA((2 * len(plan),)),
        ],
        compiler_params=pltpu.CompilerParams(vmem_limit_bytes=16 << 20),
        cost_estimate=pl.CostEstimate(
            flops=terms * rows * width, bytes_accessed=4 * terms * rows * width, transcendentals=0
        ),
    )(*sources)


def two_sums(first, second):
    shape = first[0].shape
    plan = (((((0, 0), (1, 0))), 0, 0), ((((2, 0), (3, 0))), 1, 0))
    return sums(plan, [*first, *second], shape[0], [shape, shape])


def loss_kernel(offsets, replicas, pair_dev, where_ref, *refs):
    unit_refs, refs = refs[:-7], refs[-7:]
    fresh_ref, other_ref, target_ref, query_ref, pin_ref, grad_query, grad_pin = refs
    me, section = where_ref[0], where_ref[1]
    sections = len(offsets)
    width = grad_query.shape[1]
    pairs = replicas * pair_dev

    def numbers(shape, dim):
        return lax.broadcasted_iota(jnp.int32, shape, dim)

    units = []
    for ref in unit_refs:
        count = ref.shape[0] // (2 * pairs)
        units += [ref.at[pl.ds(2 * pairs * i, 2 * pairs)] for i in range(count)]

    fresh = fresh_ref[...] + other_ref[other_ref.shape[0] - fresh_ref.shape[0] :]
    row = numbers((sections * replicas, 1), 0)
    source = (me ^ (row % replicas)) * sections
    for j, offset in enumerate(offsets):
        source = source + jnp.where(row // replicas == j, section ^ offset, 0)
    pick = (source == numbers((1, sections * replicas), 1)).astype(jnp.float32)
    fresh = jnp.dot(pick.astype(jnp.bfloat16), fresh, preferred_element_type=jnp.float32)
    squares = jnp.sum(fresh * fresh, axis=1, keepdims=True)
    squares = sum(squares[j * replicas : (j + 1) * replicas] for j in range(sections))
    fresh_length = jnp.sqrt(squares + EPSILON)

    pair = numbers((pairs, 1), 0)
    first = pair % pair_dev == 0
    spread = (pair // pair_dev == numbers((1, replicas), 1)).astype(jnp.float32)
    spread = spread.astype(jnp.bfloat16)
    cosines = jnp.zeros((pairs, pairs), jnp.float32)
    for j in range(sections):
        unit = fresh[j * replicas : (j + 1) * replicas] / fresh_length
        placed = jnp.dot(spread, unit.astype(jnp.bfloat16), preferred_element_type=jnp.float32)
        pins = jnp.where(first, placed, units[j][pairs:].astype(jnp.float32)).astype(jnp.bfloat16)
        if j == 0:
            own_unit, own_pins = unit[:1], pins
        cosines = cosines + lax.dot_general(
            units[j][:pairs], pins, (((1,), (1,)), ((), ())), preferred_element_type=jnp.float32
        )
    raised = jnp.exp(INV_TEMP * cosines - INV_TEMP)
    probs = raised / jnp.sum(raised, axis=1, keepdims=True)
    column = numbers((1, pairs), 1)
    pin_number = (me ^ (column // pair_dev)) * pair_dev + column % pair_dev
    onehot = (pin_number == target_ref[...]).astype(jnp.float32)
    weights = ((probs - onehot) * INV_TEMP).astype(jnp.bfloat16)
    floats = weights.astype(jnp.float32)
    dots = floats * cosines
    query_dot = jnp.sum(dots[:pair_dev], axis=1, keepdims=True)
    pin_dot = jnp.sum(dots.T[:pair_dev], axis=1, keepdims=True)
    query_step = jnp.dot(weights[:pair_dev], own_pins, preferred_element_type=jnp.float32)
    pin_step = jnp.dot(
        floats.T[:pair_dev].astype(jnp.bfloat16),
        units[0][:pairs],
        preferred_element_type=jnp.float32,
    )
    columns = pl.ds(pl.multiple_of(section * width, 128), width)
    for ref, step, dot, grad, fresh_first in (
        (query_ref, query_step, query_dot, grad_query, False),
        (pin_ref, pin_step, pin_dot, grad_pin, True),
    ):
        whole = ref[...].astype(jnp.float32)
        length = jnp.sqrt(jnp.sum(whole * whole, axis=1, keepdims=True) + EPSILON)
        unit = ref[:, columns].astype(jnp.float32) / length
        if fresh_first:
            is_first = numbers((pair_dev, 1), 0) == 0
            length = jnp.where(is_first, fresh_length[:1], length)
            unit = jnp.where(is_first, own_unit, unit)
        grad[...] = (step - unit * dot) / length


def local(held, norm_gain, w_gate, w_up, w_down, layer_counts, query_bank, pin_bank, positive):
    replicas = lax.axis_size("dp")
    sections = lax.axis_size("section")
    rows_dev, model_width = held.shape[1:]
    pair_dev = query_bank.shape[0]
    half = replicas // 2
    cut = rows_dev // 2
    order = ring_order(replicas)
    place = [order.index(replica) for replica in range(replicas)]
    ring = [(order[i], order[(i + 1) % replicas]) for i in range(replicas)]
    ring_back = [(b, a) for a, b in ring]
    me = lax.axis_index("dp")
    section = lax.axis_index("section")
    position = jnp.where(me % 2 == 0, me // 2, replicas - (me + 1) // 2)
    turn = (replicas - position).astype(jnp.uint32)
    last = sections - 1
    active = layer_counts[0] > 0
    stream = held[0]
    col_width = model_width // sections
    col_start = (section * col_width).astype(jnp.uint32)
    turn, position, col_start = lax.optimization_barrier((turn, position, col_start))

    def forward(values):
        return lax.ppermute(values, "dp", ring)

    def backward(values):
        return lax.ppermute(values, "dp", ring_back)

    def own_columns(values):
        return lax.dynamic_slice(values, (jnp.uint32(0), col_start), (values.shape[0], col_width))

    def after(values, others):
        return lax.optimization_barrier((values, others))[0]

    def doubled(values, reach):
        others = lax.ppermute(values, "dp", [(i, i ^ reach) for i in range(replicas)])
        return tuple(jnp.concatenate([v, o], axis=v.ndim - 2) for v, o in zip(values, others))

    def gathered(values, reach):
        while reach < replicas:
            values = doubled(values, reach)
            reach *= 2
        return values

    def added_up(values):
        reach = 1
        while reach < replicas:
            pairs = [(i * sections + last, (i ^ reach) * sections + last) for i in range(replicas)]
            values = values + lax.ppermute(values, BOTH, pairs)
            reach *= 2
        return values

    def with_held(rows):
        rows = jnp.concatenate([rows, rows])
        rows = lax.dynamic_slice(rows, (turn, jnp.uint32(0)), (replicas, model_width))
        mine = jnp.arange(replicas)[:, None] == position
        return rows + jnp.where(mine, stream[rows_dev - 1 :].astype(jnp.float32), 0.0)

    def unit_columns():
        query_send = unit_rows(query_bank)[0].astype(jnp.bfloat16)
        pin_send = unit_rows(pin_bank)[0].astype(jnp.bfloat16)
        return jnp.stack([own_columns(query_send), own_columns(pin_send)]), positive[:, None]

    def gather_and_multiply():
        normed = rms_scaled(stream, norm_gain[0])
        f_top, f_low = normed[:cut], normed[cut:]
        b_top, b_low = f_top, f_low
        f_top, b_low = forward(f_top), backward(b_low)
        f_low, b_top = forward(f_low), backward(b_top)
        own, tails, weights = multiply(
            [normed[:cut], normed[cut:]], [w_gate[0, 0], w_up[0, 0], w_down[0, 0]], True
        )
        sends = doubled(unit_columns(), 1)
        reach = 2
        ready = (own, sends)
        terms_f, terms_b, rows_f, rows_b = [], [], [], [tails[1:2]]
        for step in range(1, half):
            arrived = [f_top, f_low, b_top, b_low]
            f_top, b_low = after((f_top, b_low), ready)
            f_top, b_low = forward(f_top), backward(b_low)
            if step < half - 1:
                f_low, b_top = after((f_low, b_top), ready)
                f_low, b_top = forward(f_low), backward(b_top)
            if reach < replicas:
                sends = doubled(after(sends, arrived), reach)
                reach *= 2
            terms, tails = multiply(arrived, weights, False)
            terms_f.append(terms[:2])
            terms_b.append(terms[2:])
            rows_f.append(tails[1:2])
            rows_b.append(tails[3:4])
            ready = (terms, sends)
        sends = gathered(sends, reach)
        f_low, b_top = forward(terms_b[-1][1]), backward(terms_f[-1][0])
        far, tails = multiply([f_top, b_low], weights, False)
        f_top, b_low = forward(far[0]), backward(far[1])
        rows = jnp.concatenate(rows_b + [tails[1:2]] + rows_f[::-1])
        rows = after(rows, (f_low, b_top))
        fresh = added_up(with_held(rows)).astype(jnp.bfloat16)
        moving = (f_top, f_low, b_top, b_low)
        return tuple(own), tuple(terms_f), tuple(terms_b), moving, fresh, sends

    def gather_only():
        fresh = added_up(with_held(jnp.zeros((replicas, model_width), jnp.float32)))
        empty = jnp.zeros((cut, model_width), jnp.bfloat16)
        some = tuple((empty, empty) for _ in range(1, half))
        return (
            (empty, empty),
            some,
            some,
            (empty,) * 4,
            fresh.astype(jnp.bfloat16),
            gathered(unit_columns(), 1),
        )

    own, terms_f, terms_b, moving, fresh, sends = lax.cond(
        active, gather_and_multiply, gather_only
    )

    sends, targets = sends
    pairs = sends.shape[1]
    fresh = jnp.stack([fresh[place[replica]] for replica in range(replicas)])
    fresh = jnp.where(section == last, fresh, jnp.zeros_like(fresh))
    fresh = fresh.reshape(replicas * sections, col_width)
    units = sends.reshape(2 * pairs, col_width)

    def section_swap(units, fresh, reach):
        message = jnp.concatenate([units, fresh])
        other = lax.ppermute(message, "section", [(s, s ^ reach) for s in range(sections)])
        return other

    offsets = [0, sections // 2]
    other = section_swap(units, fresh, sections // 2)

    def reduce_middle(moving):
        f_top, f_low, b_top, b_low = moving
        for distance in range(half - 1, 1, -1):
            to_f, to_b = terms_b[distance - 1], terms_f[distance - 1]
            if distance < half - 1:
                f_low, b_top = two_sums((to_f[1], f_low), (to_b[0], b_top))
                f_low, b_top = forward(f_low), backward(b_top)
            f_top, b_low = two_sums((to_f[0], f_top), (to_b[1], b_low))
            f_top, b_low = forward(f_top), backward(b_low)
        return f_top, f_low, b_top, b_low

    moving = lax.cond(active, reduce_middle, lambda moving: moving, moving)
    other, moving = lax.optimization_barrier((other, moving))
    units = [units]
    reach = sections // 4
    while reach:
        size = other.shape[0] - fresh.shape[0]
        units, fresh = units + [other[:size]], fresh + other[size:]
        other = section_swap(jnp.concatenate(units), fresh, reach)
        offsets += [offset ^ reach for offset in offsets]
        reach //= 2
    place_here = jnp.stack([me, section])

    def loss(units, fresh, other):
        grad = jax.ShapeDtypeStruct((pair_dev, col_width), jnp.float32)
        return pl.pallas_call(
            functools.partial(loss_kernel, offsets, replicas, pair_dev),
            out_shape=[grad, grad],
            in_specs=[pl.BlockSpec(memory_space=pltpu.SMEM)] + [IN_VMEM] * (len(units) + 6),
            out_specs=[IN_VMEM] * 2,
            compiler_params=pltpu.CompilerParams(vmem_limit_bytes=32 << 20),
        )(place_here, *units, other, fresh, other, targets, query_bank, pin_bank)

    def reduce_last(moving, units, fresh, other):
        f_top, f_low, b_top, b_low = moving
        to_f, to_b = terms_b[0], terms_f[0]
        f_low, b_top = two_sums((to_f[1], f_low), (to_b[0], b_top))
        f_low, b_top = forward(f_low), backward(b_top)
        f_top, b_low = two_sums((to_f[0], f_top), (to_b[1], b_low))
        f_top, b_low = forward(f_top), backward(b_low)
        grads = loss(units, fresh, other)
        plan = (
            (((0, 0), (1, 0), (3, 0), (5, 0)), 0, 0),
            (((0, cut), (2, 0), (4, 0), (6, 0)), 0, cut),
        )
        sources = [stream, *own, f_top, f_low, b_top, b_low]
        return *sums(plan, sources, cut, [stream.shape]), *grads

    def keep_stream(moving, units, fresh, other):
        return stream + jnp.concatenate(own), *loss(units, fresh, other)

    stream_out, grad_query, grad_pin = lax.cond(active, reduce_last, keep_stream, moving, units, fresh, other)
    return (stream_out[None], grad_query, grad_pin)


def solution(mesh):
    return jax.shard_map(
        local,
        mesh=mesh,
        in_specs=(
            P("section", "dp", None),
            P("section", None, None),
            P("section", None, None, "dp"),
            P("section", None, None, "dp"),
            P("section", None, "dp", None),
            P("section"),
            P("dp", None),
            P("dp", None),
            P("dp"),
        ),
        out_specs=(P("section", "dp", None), P("dp", "section"), P("dp", "section")),
        check_vma=False,
    )
```

```python
import functools

import jax
import jax.numpy as jnp
from jax import lax
from jax.experimental import pallas as pl
from jax.experimental.pallas import tpu as pltpu
from jax.sharding import PartitionSpec as P

INV_TEMP = 20.0
EPSILON = 1e-06
BOTH = ("dp", "section")
ANYWHERE = pl.BlockSpec(memory_space=pl.ANY)
IN_VMEM = pl.BlockSpec(memory_space=pltpu.VMEM)


def ring_order(size):
    return list(range(0, size, 2)) + list(range(size - 1, 0, -2))


def unit_rows(values):
    floats = values.astype(jnp.float32)
    length = jnp.sqrt(jnp.sum(floats * floats, axis=-1, keepdims=True) + EPSILON)
    return (floats / length, length)


def copies_in(pieces, tokens, sems):
    rows = pieces[0].shape[0]
    copies = [
        pltpu.make_async_copy(piece, tokens.at[pl.ds(i * rows, rows)], sems.at[i])
        for i, piece in enumerate(pieces)
    ]
    for copy in copies:
        copy.start()
    return copies


def copies_out(result, outs, sems):
    rows = outs[0].shape[0]
    copies = [
        pltpu.make_async_copy(result.at[pl.ds(i * rows, rows)], out, sems.at[i])
        for i, out in enumerate(outs)
    ]
    for copy in copies:
        copy.start()
    for copy in copies:
        copy.wait()


def gated(tokens, gate, up, hidden):
    gate_out = jnp.dot(tokens[...], gate[...], preferred_element_type=jnp.float32)
    up_out = jnp.dot(tokens[...], up[...], preferred_element_type=jnp.float32)
    hidden[...] = (gate_out / (1 + jnp.exp(-gate_out)) * up_out).astype(jnp.bfloat16)


def lowered(hidden, down, result):
    result[...] = jnp.dot(hidden[...], down[...], preferred_element_type=jnp.float32).astype(
        jnp.bfloat16
    )


def last_rows(result, count, tails):
    rows = result.shape[0] // count
    for i in range(count):
        end = result[(i + 1) * rows - 16 : (i + 1) * rows].astype(jnp.float32)
        tails[i : i + 1] = end[15:]


def first_kernel(count, *refs):
    pieces, weights, refs = refs[:count], refs[count : count + 3], refs[count + 3 :]
    outs, tails, kept, refs = refs[:count], refs[count], refs[count + 1 : count + 4], refs[count + 4 :]
    tokens, hidden, result, in_sems, out_sems, weight_sems = refs
    loads = copies_in(pieces, tokens, in_sems)
    fetches = [
        pltpu.make_async_copy(weight, keep, weight_sems.at[i])
        for i, (weight, keep) in enumerate(zip(weights, kept))
    ]
    for copy in fetches:
        copy.start()
    for copy in loads + fetches[:2]:
        copy.wait()
    gated(tokens, kept[0], kept[1], hidden)
    fetches[2].wait()
    lowered(hidden, kept[2], result)
    last_rows(result, count, tails)
    copies_out(result, outs, out_sems)


def next_kernel(count, *refs):
    pieces, weights, refs = refs[:count], refs[count : count + 3], refs[count + 3 :]
    outs, tails, refs = refs[:count], refs[count], refs[count + 1 :]
    tokens, hidden, result, in_sems, out_sems = refs
    for copy in copies_in(pieces, tokens, in_sems):
        copy.wait()
    gated(tokens, weights[0], weights[1], hidden)
    lowered(hidden, weights[2], result)
    last_rows(result, count, tails)
    copies_out(result, outs, out_sems)


def multiply(pieces, weights, keep):
    count = len(pieces)
    rows, width = pieces[0].shape
    units = weights[0].shape[1]
    scratch = [
        pltpu.VMEM((count * rows, width), jnp.bfloat16),
        pltpu.VMEM((count * rows, units), jnp.bfloat16),
        pltpu.VMEM((count * rows, width), jnp.bfloat16),
        pltpu.SemaphoreType.DMA((count,)),
        pltpu.SemaphoreType.DMA((count,)),
    ]
    out_shape = [jax.ShapeDtypeStruct(p.shape, jnp.bfloat16) for p in pieces]
    out_shape += [jax.ShapeDtypeStruct((8, width), jnp.float32)]
    params = pltpu.CompilerParams(vmem_limit_bytes=20 << 20)
    tokens = count * rows
    cost = pl.CostEstimate(
        flops=6 * tokens * width * units, bytes_accessed=4 * tokens * width, transcendentals=0
    )
    if keep:
        outs = pl.pallas_call(
            functools.partial(first_kernel, count),
            out_shape=out_shape + [pltpu.VMEM(w.shape, w.dtype) for w in weights],
            in_specs=[ANYWHERE] * (count + 3),
            out_specs=[ANYWHERE] * count + [IN_VMEM] * 4,
            scratch_shapes=scratch + [pltpu.SemaphoreType.DMA((3,))],
            compiler_params=params,
            cost_estimate=cost,
        )(*pieces, *weights)
        return outs[:count], outs[count], outs[count + 1 :]
    weights = [pltpu.with_memory_space_constraint(w, pltpu.VMEM) for w in weights]
    outs = pl.pallas_call(
        functools.partial(next_kernel, count),
        out_shape=out_shape,
        in_specs=[ANYWHERE] * count + [IN_VMEM] * 3,
        out_specs=[ANYWHERE] * count + [IN_VMEM],
        scratch_shapes=scratch,
        compiler_params=params,
        cost_estimate=cost,
    )(*pieces, *weights)
    return outs[:count], outs[count]


def norm_kernel(parts, stream, gain, top, low, loaded, result, in_sems, out_sems):
    rows = stream.shape[0] // parts
    loads = []
    for i in range(parts):
        here = pl.ds(i * rows, rows)
        loads.append(pltpu.make_async_copy(stream.at[here], loaded.at[here], in_sems.at[i]))
        loads[-1].start()
    scale = gain[...].astype(jnp.float32)
    stores = []
    for i in range(parts):
        loads[i].wait()
        values = loaded[i * rows : (i + 1) * rows].astype(jnp.float32)
        mean = jnp.mean(values * values, axis=1, keepdims=True)
        values = values * lax.rsqrt(mean + EPSILON) * scale
        result[i * rows : (i + 1) * rows] = values.astype(jnp.bfloat16)
        out, row = (top, i * rows) if i < parts // 2 else (low, (i - parts // 2) * rows)
        store = pltpu.make_async_copy(
            result.at[pl.ds(i * rows, rows)], out.at[pl.ds(row, rows)], out_sems.at[i]
        )
        store.start()
        stores.append(store)
    for store in stores:
        store.wait()


def normalized(stream, gain):
    rows, width = stream.shape
    parts = 4
    out = jax.ShapeDtypeStruct((rows // 2, width), jnp.bfloat16)
    return pl.pallas_call(
        functools.partial(norm_kernel, parts),
        out_shape=[out, out],
        in_specs=[ANYWHERE, IN_VMEM],
        out_specs=[ANYWHERE] * 2,
        scratch_shapes=[
            pltpu.VMEM((rows, width), jnp.bfloat16),
            pltpu.VMEM((rows, width), jnp.bfloat16),
            pltpu.SemaphoreType.DMA((parts,)),
            pltpu.SemaphoreType.DMA((parts,)),
        ],
        compiler_params=pltpu.CompilerParams(vmem_limit_bytes=16 << 20),
    )(stream, gain)


def sum_kernel(plan, sources, *refs):
    ins, outs, (loaded, result, in_sems, out_sems) = refs[:sources], refs[sources:-4], refs[-4:]
    rows = result.shape[1]
    part = rows // 2
    groups, slot = [], 0
    for group, (terms, out, out_row) in enumerate(plan):
        for cut in range(2):
            copies = []
            for i, (source, row) in enumerate(terms):
                copies.append(
                    pltpu.make_async_copy(
                        ins[source].at[pl.ds(row + cut * part, part)],
                        loaded.at[slot + i, pl.ds(cut * part, part)],
                        in_sems.at[2 * (slot + i) + cut],
                    )
                )
            groups.append((group, cut, slot, copies, out, out_row))
        slot += len(terms)
    for entry in groups:
        for copy in entry[3]:
            copy.start()
    stores = []
    for group, cut, slot, copies, out, out_row in groups:
        for copy in copies:
            copy.wait()
        here = slice(cut * part, (cut + 1) * part)
        total = loaded[slot, here].astype(jnp.float32)
        for i in range(1, len(copies)):
            total = total + loaded[slot + i, here].astype(jnp.float32)
        result[group, here] = total.astype(jnp.bfloat16)
        store = pltpu.make_async_copy(
            result.at[group, pl.ds(cut * part, part)],
            outs[out].at[pl.ds(out_row + cut * part, part)],
            out_sems.at[2 * group + cut],
        )
        store.start()
        stores.append(store)
    for store in stores:
        store.wait()


def sums(plan, sources, rows, out_shapes, kind=jax.ShapeDtypeStruct):
    terms = sum(len(entry[0]) for entry in plan)
    width = sources[0].shape[1]
    return pl.pallas_call(
        functools.partial(sum_kernel, plan, len(sources)),
        out_shape=[kind(shape, jnp.bfloat16) for shape in out_shapes],
        in_specs=[ANYWHERE] * len(sources),
        out_specs=[ANYWHERE] * len(out_shapes),
        scratch_shapes=[
            pltpu.VMEM((terms, rows, width), jnp.bfloat16),
            pltpu.VMEM((len(plan), rows, width), jnp.bfloat16),
            pltpu.SemaphoreType.DMA((2 * terms,)),
            pltpu.SemaphoreType.DMA((2 * len(plan),)),
        ],
        compiler_params=pltpu.CompilerParams(vmem_limit_bytes=16 << 20),
        cost_estimate=pl.CostEstimate(
            flops=terms * rows * width, bytes_accessed=4 * terms * rows * width, transcendentals=0
        ),
    )(*sources)


def two_sums(first, second):
    shape = first[0].shape
    plan = (((((0, 0), (1, 0))), 0, 0), ((((2, 0), (3, 0))), 1, 0))
    return sums(plan, [*first, *second], shape[0], [shape, shape])


def rows_kernel(slots, position, stream, *refs):
    tails, out = refs[:-1], refs[-1]
    for offset, (source, slot) in enumerate(slots):
        row = tails[source][slot : slot + 1]
        if offset == 0:
            row = row + stream[...].astype(jnp.float32)[15:]
        out[pl.ds(lax.rem(position[0] + offset, len(slots)), 1)] = row


def ring_rows(slots, tails, position, stream):
    width = stream.shape[1]
    last_block = stream.shape[0] // 16 - 1
    shape = (len(slots), width)
    return pl.pallas_call(
        functools.partial(rows_kernel, slots),
        grid=(1,),
        out_shape=jax.ShapeDtypeStruct(shape, jnp.float32),
        in_specs=[
            pl.BlockSpec(memory_space=pltpu.SMEM),
            pl.BlockSpec((16, width), lambda i: (last_block, 0)),
        ]
        + [pl.BlockSpec((8, width), lambda i: (0, 0))] * len(tails),
        out_specs=pl.BlockSpec(shape, lambda i: (0, 0)),
    )(position, stream, *tails)


def loss_kernel(offsets, replicas, pair_dev, where_ref, *refs):
    known, (query_ref, pin_ref, grad_query, grad_pin) = refs[:-4], refs[-4:]
    me, section = where_ref[0], where_ref[1]
    sections = len(offsets)
    width = grad_query.shape[1]
    pairs = replicas * pair_dev

    def numbers(shape, dim):
        return lax.broadcasted_iota(jnp.int32, shape, dim)

    size = 2 * pairs + sections * replicas
    units = [
        ref.at[pl.ds(size * i, size)] for ref in known for i in range(ref.shape[0] // size)
    ]

    fresh = sum(unit[2 * pairs :].astype(jnp.float32) for unit in units).astype(jnp.bfloat16)
    row = numbers((sections * replicas, 1), 0)
    replica = me ^ (row % replicas)
    source = jnp.where(replica % 2 == 0, replica // 2, replicas - (replica + 1) // 2) * sections
    for j, offset in enumerate(offsets):
        source = source + jnp.where(row // replicas == j, section ^ offset, 0)
    pick = (source == numbers((1, sections * replicas), 1)).astype(jnp.float32)
    fresh = jnp.dot(pick.astype(jnp.bfloat16), fresh, preferred_element_type=jnp.float32)
    squares = jnp.sum(fresh * fresh, axis=1, keepdims=True)
    squares = sum(squares[j * replicas : (j + 1) * replicas] for j in range(sections))
    fresh_length = jnp.sqrt(squares + EPSILON)

    pair = numbers((pairs, 1), 0)
    first = pair % pair_dev == 0
    spread = (pair // pair_dev == numbers((1, replicas), 1)).astype(jnp.float32)
    spread = spread.astype(jnp.bfloat16)
    cosines = jnp.zeros((pairs, pairs), jnp.float32)
    for j in range(sections):
        unit = fresh[j * replicas : (j + 1) * replicas] / fresh_length
        placed = jnp.dot(spread, unit.astype(jnp.bfloat16), preferred_element_type=jnp.float32)
        pins = jnp.where(first, placed, units[j][pairs : 2 * pairs].astype(jnp.float32)).astype(jnp.bfloat16)
        if j == 0:
            own_unit, own_pins = unit[:1], pins
        cosines = cosines + lax.dot_general(
            units[j][:pairs], pins, (((1,), (1,)), ((), ())), preferred_element_type=jnp.float32
        )
    raised = jnp.exp(INV_TEMP * cosines - INV_TEMP)
    probs = raised / jnp.sum(raised, axis=1, keepdims=True)
    column = numbers((1, pairs), 1)
    pin_number = (me ^ (column // pair_dev)) * pair_dev + column % pair_dev
    ahead = (pair // pair_dev * pair_dev == column).astype(jnp.float32).astype(jnp.bfloat16)
    targets = jnp.dot(
        ahead, units[0][pairs : 2 * pairs, :128], preferred_element_type=jnp.float32
    )
    is_own = pair % pair_dev == numbers((1, 128), 1)
    target = jnp.sum(jnp.where(is_own, targets, 0.0), axis=1, keepdims=True)
    onehot = (pin_number.astype(jnp.float32) == target).astype(jnp.float32)
    weights = ((probs - onehot) * INV_TEMP).astype(jnp.bfloat16)
    floats = weights.astype(jnp.float32)
    dots = floats * cosines
    query_dot = jnp.sum(dots[:pair_dev], axis=1, keepdims=True)
    pin_dot = jnp.sum(dots.T[:pair_dev], axis=1, keepdims=True)
    query_step = jnp.dot(weights[:pair_dev], own_pins, preferred_element_type=jnp.float32)
    pin_step = jnp.dot(
        floats.T[:pair_dev].astype(jnp.bfloat16),
        units[0][:pairs],
        preferred_element_type=jnp.float32,
    )
    columns = pl.ds(pl.multiple_of(section * width, 128), width)
    for ref, step, dot, grad, fresh_first in (
        (query_ref, query_step, query_dot, grad_query, False),
        (pin_ref, pin_step, pin_dot, grad_pin, True),
    ):
        whole = ref[...].astype(jnp.float32)
        length = jnp.sqrt(jnp.sum(whole * whole, axis=1, keepdims=True) + EPSILON)
        unit = ref[:, columns].astype(jnp.float32) / length
        if fresh_first:
            is_first = numbers((pair_dev, 1), 0) == 0
            length = jnp.where(is_first, fresh_length[:1], length)
            unit = jnp.where(is_first, own_unit, unit)
        grad[...] = (step - unit * dot) / length


def local(held, norm_gain, w_gate, w_up, w_down, layer_counts, query_bank, pin_bank, positive):
    replicas = lax.axis_size("dp")
    sections = lax.axis_size("section")
    rows_dev, model_width = held.shape[1:]
    pair_dev = query_bank.shape[0]
    half = replicas // 2
    cut = rows_dev // 2
    order = ring_order(replicas)
    ring = [(order[i], order[(i + 1) % replicas]) for i in range(replicas)]
    ring_back = [(b, a) for a, b in ring]
    me = lax.axis_index("dp")
    section = lax.axis_index("section")
    position = jnp.where(me % 2 == 0, me // 2, replicas - (me + 1) // 2)
    position = position.reshape(1)
    last = sections - 1
    active = layer_counts[0] > 0
    stream = held[0]
    col_width = model_width // sections
    col_start = (section * col_width).astype(jnp.uint32)
    position, col_start = lax.optimization_barrier((position, col_start))

    def forward(values):
        return lax.ppermute(values, "dp", ring)

    def backward(values):
        return lax.ppermute(values, "dp", ring_back)

    def own_columns(values):
        return lax.dynamic_slice(values, (jnp.uint32(0), col_start), (values.shape[0], col_width))

    def after(values, others):
        return lax.optimization_barrier((values, others))[0]

    def doubled(values, reach):
        other = lax.ppermute(values, "dp", [(i, i ^ reach) for i in range(replicas)])
        return jnp.concatenate([values, other], axis=1)

    def gathered(values, reach):
        while reach < replicas:
            values = doubled(values, reach)
            reach *= 2
        return values

    def added_up(values):
        reach = 1
        while reach < replicas:
            pairs = [(i * sections + last, (i ^ reach) * sections + last) for i in range(replicas)]
            values = values + lax.ppermute(values, BOTH, pairs)
            reach *= 2
        return values

    def unit_columns(query_bank, pin_bank):
        query_send = unit_rows(query_bank)[0].astype(jnp.bfloat16)
        pin_send = own_columns(unit_rows(pin_bank)[0].astype(jnp.bfloat16))
        numbers = jnp.pad(positive, (0, col_width - pair_dev)).astype(jnp.bfloat16)
        is_first = (jnp.arange(pair_dev) == 0)[:, None]
        return jnp.stack([own_columns(query_send), jnp.where(is_first, numbers, pin_send)])

    def gather_and_multiply():
        f_top, f_low = normalized(stream, norm_gain[0])
        b_top, b_low = f_top, f_low
        first = [f_top, f_low]
        f_top, b_low = forward(f_top), backward(b_low)
        f_low, b_top = forward(f_low), backward(b_top)
        own, tails, weights = multiply(
            first, [w_gate[0, 0], w_up[0, 0], w_down[0, 0]], True
        )
        sends = unit_columns(*after((query_bank, pin_bank), own))
        reach = 1
        ready_near, ready_far = own, own
        terms_f, terms_b, all_tails = [], [], [tails]
        for step in range(1, half):
            near, rest = (f_top, b_low), (f_low, b_top)
            f_top, b_low = after(near, ready_near)
            f_top, b_low = forward(f_top), backward(b_low)
            (tf_top, tb_low), near_tails = multiply(near, weights, False)
            ready_far = (tf_top, tb_low, ready_far)
            if step < half - 1:
                f_low, b_top = after(rest, ready_far)
                f_low, b_top = forward(f_low), backward(b_top)
            else:
                tf_send, tb_send = after((tf_top, tb_low), ready_far)
                f_low, b_top = forward(tb_send), backward(tf_send)
            if reach < replicas:
                sends = doubled(after(sends, near), reach)
                reach *= 2
            ready_far = sends
            (tf_low, tb_top), rest_tails = multiply(rest, weights, False)
            ready_near = (tf_low, tb_top)
            terms_f.append((tf_top, tf_low))
            terms_b.append((tb_top, tb_low))
            all_tails += [near_tails, rest_tails]
        sends = gathered(sends, reach)
        far, tails = multiply([f_top, b_low], weights, False)
        f_top, b_low = forward(far[0]), backward(far[1])
        (f_top, b_low), sends = lax.optimization_barrier(((f_top, b_low), sends))
        f_top, b_low = two_sums((terms_b[-1][0], f_top), (terms_f[-1][1], b_low))
        all_tails.append(tails)
        slots = (
            [(0, 1)]
            + [(2 * step - 1, 1) for step in range(1, half)]
            + [(2 * half - 1, 1)]
            + [(2 * step, 0) for step in range(half - 1, 0, -1)]
        )
        all_tails = after(all_tails, (f_top, b_low))
        f_top, b_low = forward(f_top), backward(b_low)
        rows = ring_rows(slots, all_tails, position, stream)
        fresh = added_up(rows).astype(jnp.bfloat16)
        moving = (f_top, f_low, b_top, b_low)
        return tuple(own), tuple(terms_f), tuple(terms_b), moving, fresh, sends

    def gather_only():
        fresh = added_up(
            ring_rows([(0, 0)] * replicas, [jnp.zeros((8, model_width), jnp.float32)], position, stream)
        )
        empty = jnp.zeros((cut, model_width), jnp.bfloat16)
        some = tuple((empty, empty) for _ in range(1, half))
        return (
            (empty, empty),
            some,
            some,
            (empty,) * 4,
            fresh.astype(jnp.bfloat16),
            gathered(unit_columns(query_bank, pin_bank), 1),
        )

    own, terms_f, terms_b, moving, fresh, sends = lax.cond(
        active, gather_and_multiply, gather_only
    )

    pairs = sends.shape[1]
    fresh = jnp.where(section == last, fresh, jnp.zeros_like(fresh))
    fresh = fresh.reshape(replicas * sections, col_width)
    known = [jnp.concatenate([sends.reshape(2 * pairs, col_width), fresh])]
    offsets = [0]

    def section_swap(reach):
        offsets.extend([offset ^ reach for offset in offsets])
        message = known[0] if len(known) == 1 else jnp.concatenate(known)
        other = lax.ppermute(message, "section", [(s, s ^ reach) for s in range(sections)])
        known.append(other)

    section_swap(sections // 2)

    def reduce_middle(moving):
        f_top, f_low, b_top, b_low = moving
        for distance in range(half - 2, 1, -1):
            to_f, to_b = terms_b[distance - 1], terms_f[distance - 1]
            f_low, b_top = two_sums((to_f[1], f_low), (to_b[0], b_top))
            f_low, b_top = forward(f_low), backward(b_top)
            f_top, b_low = two_sums((to_f[0], f_top), (to_b[1], b_low))
            f_top, b_low = forward(f_top), backward(b_low)
        return f_top, f_low, b_top, b_low

    moving = lax.cond(active, reduce_middle, lambda moving: moving, moving)
    known[1], moving = lax.optimization_barrier((known[1], moving))
    reach = sections // 4
    while reach:
        section_swap(reach)
        reach //= 2
    place_here = jnp.stack([me, section])

    def loss(known):
        grad = jax.ShapeDtypeStruct((pair_dev, col_width), jnp.float32)
        return pl.pallas_call(
            functools.partial(loss_kernel, offsets, replicas, pair_dev),
            out_shape=[grad, grad],
            in_specs=[pl.BlockSpec(memory_space=pltpu.SMEM)] + [IN_VMEM] * (len(known) + 2),
            out_specs=[IN_VMEM] * 2,
            compiler_params=pltpu.CompilerParams(vmem_limit_bytes=32 << 20),
        )(place_here, *known, query_bank, pin_bank)

    def reduce_last(moving, known):
        f_top, f_low, b_top, b_low = moving
        to_f, to_b = terms_b[0], terms_f[0]
        f_low, b_top = two_sums((to_f[1], f_low), (to_b[0], b_top))
        f_low, b_top = forward(f_low), backward(b_top)
        f_top, b_low = two_sums((to_f[0], f_top), (to_b[1], b_low))
        f_top, b_low = forward(f_top), backward(b_low)
        grads = loss(known)
        plan = (
            (((0, 0), (1, 0), (3, 0), (5, 0)), 0, 0),
            (((0, cut), (2, 0), (4, 0), (6, 0)), 0, cut),
        )
        sources = [stream, *own, f_top, f_low, b_top, b_low]
        return *sums(plan, sources, cut, [stream.shape], pltpu.HBM), *grads

    def keep_stream(moving, known):
        return stream + jnp.concatenate(own), *loss(known)

    stream_out, grad_query, grad_pin = lax.cond(active, reduce_last, keep_stream, moving, known)
    return (stream_out[None], grad_query, grad_pin)


def solution(mesh):
    return jax.shard_map(
        local,
        mesh=mesh,
        in_specs=(
            P("section", "dp", None),
            P("section", None, None),
            P("section", None, None, "dp"),
            P("section", None, None, "dp"),
            P("section", None, "dp", None),
            P("section"),
            P("dp", None),
            P("dp", None),
            P("dp"),
        ),
        out_specs=(P("section", "dp", None), P("dp", "section"), P("dp", "section")),
        check_vma=False,
    )
```

```python
import functools

import jax
import jax.numpy as jnp
from jax import lax
from jax.experimental import pallas as pl
from jax.experimental.pallas import tpu as pltpu
from jax.sharding import PartitionSpec as P

INV_TEMP = 20.0
EPSILON = 1e-06
BOTH = ("dp", "section")
ANYWHERE = pl.BlockSpec(memory_space=pl.ANY)
IN_VMEM = pl.BlockSpec(memory_space=pltpu.VMEM)


def ring_order(size):
    return list(range(0, size, 2)) + list(range(size - 1, 0, -2))


def unit_rows(values):
    floats = values.astype(jnp.float32)
    length = jnp.sqrt(jnp.sum(floats * floats, axis=-1, keepdims=True) + EPSILON)
    return (floats / length, length)


def copies_in(pieces, tokens, sems):
    rows = pieces[0].shape[0]
    copies = [
        pltpu.make_async_copy(piece, tokens.at[pl.ds(i * rows, rows)], sems.at[i])
        for i, piece in enumerate(pieces)
    ]
    for copy in copies:
        copy.start()
    return copies


def copies_out(result, outs, sems):
    rows = outs[0].shape[0]
    copies = [
        pltpu.make_async_copy(result.at[pl.ds(i * rows, rows)], out, sems.at[i])
        for i, out in enumerate(outs)
    ]
    for copy in copies:
        copy.start()
    for copy in copies:
        copy.wait()


def gated(tokens, gate, up, hidden):
    gate_out = jnp.dot(tokens[...], gate[...], preferred_element_type=jnp.float32)
    up_out = jnp.dot(tokens[...], up[...], preferred_element_type=jnp.float32)
    hidden[...] = (gate_out / (1 + jnp.exp(-gate_out)) * up_out).astype(jnp.bfloat16)


def lowered(hidden, down, result):
    result[...] = jnp.dot(hidden[...], down[...], preferred_element_type=jnp.float32).astype(
        jnp.bfloat16
    )


def last_rows(result, count, tails):
    rows = result.shape[0] // count
    for i in range(count):
        end = result[(i + 1) * rows - 16 : (i + 1) * rows].astype(jnp.float32)
        tails[i : i + 1] = end[15:]


def first_kernel(count, *refs):
    pieces, weights, refs = refs[:count], refs[count : count + 3], refs[count + 3 :]
    outs, tails, kept, refs = refs[:count], refs[count], refs[count + 1 : count + 4], refs[count + 4 :]
    tokens, hidden, result, in_sems, out_sems, weight_sems = refs
    loads = copies_in(pieces, tokens, in_sems)
    fetches = [
        pltpu.make_async_copy(weight, keep, weight_sems.at[i])
        for i, (weight, keep) in enumerate(zip(weights, kept))
    ]
    for copy in fetches:
        copy.start()
    for copy in loads + fetches[:2]:
        copy.wait()
    gated(tokens, kept[0], kept[1], hidden)
    fetches[2].wait()
    lowered(hidden, kept[2], result)
    last_rows(result, count, tails)
    copies_out(result, outs, out_sems)


def next_kernel(count, *refs):
    pieces, weights, refs = refs[:count], refs[count : count + 3], refs[count + 3 :]
    outs, tails, refs = refs[:count], refs[count], refs[count + 1 :]
    tokens, hidden, result, in_sems, out_sems = refs
    for copy in copies_in(pieces, tokens, in_sems):
        copy.wait()
    gated(tokens, weights[0], weights[1], hidden)
    lowered(hidden, weights[2], result)
    last_rows(result, count, tails)
    copies_out(result, outs, out_sems)


def multiply(pieces, weights, keep):
    count = len(pieces)
    rows, width = pieces[0].shape
    units = weights[0].shape[1]
    scratch = [
        pltpu.VMEM((count * rows, width), jnp.bfloat16),
        pltpu.VMEM((count * rows, units), jnp.bfloat16),
        pltpu.VMEM((count * rows, width), jnp.bfloat16),
        pltpu.SemaphoreType.DMA((count,)),
        pltpu.SemaphoreType.DMA((count,)),
    ]
    out_shape = [jax.ShapeDtypeStruct(p.shape, jnp.bfloat16) for p in pieces]
    out_shape += [jax.ShapeDtypeStruct((8, width), jnp.float32)]
    params = pltpu.CompilerParams(vmem_limit_bytes=20 << 20)
    tokens = count * rows
    cost = pl.CostEstimate(
        flops=6 * tokens * width * units, bytes_accessed=4 * tokens * width, transcendentals=0
    )
    if keep:
        outs = pl.pallas_call(
            functools.partial(first_kernel, count),
            out_shape=out_shape + [pltpu.VMEM(w.shape, w.dtype) for w in weights],
            in_specs=[ANYWHERE] * (count + 3),
            out_specs=[ANYWHERE] * count + [IN_VMEM] * 4,
            scratch_shapes=scratch + [pltpu.SemaphoreType.DMA((3,))],
            compiler_params=params,
            cost_estimate=cost,
        )(*pieces, *weights)
        return outs[:count], outs[count], outs[count + 1 :]
    weights = [pltpu.with_memory_space_constraint(w, pltpu.VMEM) for w in weights]
    outs = pl.pallas_call(
        functools.partial(next_kernel, count),
        out_shape=out_shape,
        in_specs=[ANYWHERE] * count + [IN_VMEM] * 3,
        out_specs=[ANYWHERE] * count + [IN_VMEM],
        scratch_shapes=scratch,
        compiler_params=params,
        cost_estimate=cost,
    )(*pieces, *weights)
    return outs[:count], outs[count]


def norm_kernel(parts, stream, gain, top, low, loaded, result, in_sems, out_sems):
    rows = stream.shape[0] // parts
    loads = []
    for i in range(parts):
        here = pl.ds(i * rows, rows)
        loads.append(pltpu.make_async_copy(stream.at[here], loaded.at[here], in_sems.at[i]))
        loads[-1].start()
    scale = gain[...].astype(jnp.float32)
    stores = []
    for i in range(parts):
        loads[i].wait()
        values = loaded[i * rows : (i + 1) * rows].astype(jnp.float32)
        mean = jnp.mean(values * values, axis=1, keepdims=True)
        values = values * lax.rsqrt(mean + EPSILON) * scale
        result[i * rows : (i + 1) * rows] = values.astype(jnp.bfloat16)
        out, row = (top, i * rows) if i < parts // 2 else (low, (i - parts // 2) * rows)
        store = pltpu.make_async_copy(
            result.at[pl.ds(i * rows, rows)], out.at[pl.ds(row, rows)], out_sems.at[i]
        )
        store.start()
        stores.append(store)
    for store in stores:
        store.wait()


def normalized(stream, gain):
    rows, width = stream.shape
    parts = 4
    out = jax.ShapeDtypeStruct((rows // 2, width), jnp.bfloat16)
    return pl.pallas_call(
        functools.partial(norm_kernel, parts),
        out_shape=[out, out],
        in_specs=[ANYWHERE, IN_VMEM],
        out_specs=[ANYWHERE] * 2,
        scratch_shapes=[
            pltpu.VMEM((rows, width), jnp.bfloat16),
            pltpu.VMEM((rows, width), jnp.bfloat16),
            pltpu.SemaphoreType.DMA((parts,)),
            pltpu.SemaphoreType.DMA((parts,)),
        ],
        compiler_params=pltpu.CompilerParams(vmem_limit_bytes=16 << 20),
    )(stream, gain)


def sum_kernel(plan, sources, *refs):
    ins, outs, (loaded, result, in_sems, out_sems) = refs[:sources], refs[sources:-4], refs[-4:]
    rows = result.shape[1]
    part = rows // 2
    groups, slot = [], 0
    for group, (terms, out, out_row) in enumerate(plan):
        for cut in range(2):
            copies = []
            for i, (source, row) in enumerate(terms):
                copies.append(
                    pltpu.make_async_copy(
                        ins[source].at[pl.ds(row + cut * part, part)],
                        loaded.at[slot + i, pl.ds(cut * part, part)],
                        in_sems.at[2 * (slot + i) + cut],
                    )
                )
            groups.append((group, cut, slot, copies, out, out_row))
        slot += len(terms)
    for entry in groups:
        for copy in entry[3]:
            copy.start()
    stores = []
    for group, cut, slot, copies, out, out_row in groups:
        for copy in copies:
            copy.wait()
        here = slice(cut * part, (cut + 1) * part)
        total = loaded[slot, here].astype(jnp.float32)
        for i in range(1, len(copies)):
            total = total + loaded[slot + i, here].astype(jnp.float32)
        result[group, here] = total.astype(jnp.bfloat16)
        store = pltpu.make_async_copy(
            result.at[group, pl.ds(cut * part, part)],
            outs[out].at[pl.ds(out_row + cut * part, part)],
            out_sems.at[2 * group + cut],
        )
        store.start()
        stores.append(store)
    for store in stores:
        store.wait()


def sums(plan, sources, rows, out_shapes, kind=jax.ShapeDtypeStruct):
    terms = sum(len(entry[0]) for entry in plan)
    width = sources[0].shape[1]
    return pl.pallas_call(
        functools.partial(sum_kernel, plan, len(sources)),
        out_shape=[kind(shape, jnp.bfloat16) for shape in out_shapes],
        in_specs=[ANYWHERE] * len(sources),
        out_specs=[ANYWHERE] * len(out_shapes),
        scratch_shapes=[
            pltpu.VMEM((terms, rows, width), jnp.bfloat16),
            pltpu.VMEM((len(plan), rows, width), jnp.bfloat16),
            pltpu.SemaphoreType.DMA((2 * terms,)),
            pltpu.SemaphoreType.DMA((2 * len(plan),)),
        ],
        compiler_params=pltpu.CompilerParams(vmem_limit_bytes=16 << 20),
        cost_estimate=pl.CostEstimate(
            flops=terms * rows * width, bytes_accessed=4 * terms * rows * width, transcendentals=0
        ),
    )(*sources)


def two_sums(first, second):
    shape = first[0].shape
    plan = (((((0, 0), (1, 0))), 0, 0), ((((2, 0), (3, 0))), 1, 0))
    return sums(plan, [*first, *second], shape[0], [shape, shape])


def rows_kernel(slots, position, stream, *refs):
    tails, out = refs[:-1], refs[-1]
    for offset, (source, slot) in enumerate(slots):
        row = tails[source][slot : slot + 1]
        if offset == 0:
            row = row + stream[...].astype(jnp.float32)[15:]
        out[pl.ds(lax.rem(position[0] + offset, len(slots)), 1)] = row


def ring_rows(slots, tails, position, stream):
    width = stream.shape[1]
    last_block = stream.shape[0] // 16 - 1
    shape = (len(slots), width)
    return pl.pallas_call(
        functools.partial(rows_kernel, slots),
        grid=(1,),
        out_shape=jax.ShapeDtypeStruct(shape, jnp.float32),
        in_specs=[
            pl.BlockSpec(memory_space=pltpu.SMEM),
            pl.BlockSpec((16, width), lambda i: (last_block, 0)),
        ]
        + [pl.BlockSpec((8, width), lambda i: (0, 0))] * len(tails),
        out_specs=pl.BlockSpec(shape, lambda i: (0, 0)),
    )(position, stream, *tails)


def loss_kernel(offsets, replicas, pair_dev, where_ref, *refs):
    known, (query_ref, pin_ref, grad_query, grad_pin) = refs[:-4], refs[-4:]
    me, section = where_ref[0], where_ref[1]
    sections = len(offsets)
    width = grad_query.shape[1]
    pairs = replicas * pair_dev

    def numbers(shape, dim):
        return lax.broadcasted_iota(jnp.int32, shape, dim)

    def replica_of(place):
        bits = replicas.bit_length() - 1
        return me ^ sum(((place >> k) & 1) << (bits - 1 - k) for k in range(bits))

    size = 2 * pairs + sections * replicas
    units = [
        ref.at[pl.ds(size * i, size)] for ref in known for i in range(ref.shape[0] // size)
    ]

    fresh = sum(unit[2 * pairs :].astype(jnp.float32) for unit in units).astype(jnp.bfloat16)
    row = numbers((sections * replicas, 1), 0)
    replica = replica_of(row % replicas)
    source = jnp.where(replica % 2 == 0, replica // 2, replicas - (replica + 1) // 2) * sections
    for j, offset in enumerate(offsets):
        source = source + jnp.where(row // replicas == j, section ^ offset, 0)
    pick = (source == numbers((1, sections * replicas), 1)).astype(jnp.float32)
    fresh = jnp.dot(pick.astype(jnp.bfloat16), fresh, preferred_element_type=jnp.float32)
    squares = jnp.sum(fresh * fresh, axis=1, keepdims=True)
    squares = sum(squares[j * replicas : (j + 1) * replicas] for j in range(sections))
    fresh_length = jnp.sqrt(squares + EPSILON)

    pair = numbers((pairs, 1), 0)
    first = pair % pair_dev == 0
    spread = (pair // pair_dev == numbers((1, replicas), 1)).astype(jnp.float32)
    spread = spread.astype(jnp.bfloat16)
    cosines = jnp.zeros((pairs, pairs), jnp.float32)
    for j in range(sections):
        unit = fresh[j * replicas : (j + 1) * replicas] / fresh_length
        placed = jnp.dot(spread, unit.astype(jnp.bfloat16), preferred_element_type=jnp.float32)
        pins = jnp.where(first, placed, units[j][pairs : 2 * pairs].astype(jnp.float32)).astype(jnp.bfloat16)
        if j == 0:
            own_unit, own_pins = unit[:1], pins
        cosines = cosines + lax.dot_general(
            units[j][:pairs], pins, (((1,), (1,)), ((), ())), preferred_element_type=jnp.float32
        )
    raised = jnp.exp(INV_TEMP * cosines - INV_TEMP)
    probs = raised / jnp.sum(raised, axis=1, keepdims=True)
    column = numbers((1, pairs), 1)
    pin_number = replica_of(column // pair_dev) * pair_dev + column % pair_dev
    ahead = (pair // pair_dev * pair_dev == column).astype(jnp.float32).astype(jnp.bfloat16)
    targets = jnp.dot(
        ahead, units[0][pairs : 2 * pairs, :128], preferred_element_type=jnp.float32
    )
    is_own = pair % pair_dev == numbers((1, 128), 1)
    target = jnp.sum(jnp.where(is_own, targets, 0.0), axis=1, keepdims=True)
    onehot = (pin_number.astype(jnp.float32) == target).astype(jnp.float32)
    weights = ((probs - onehot) * INV_TEMP).astype(jnp.bfloat16)
    floats = weights.astype(jnp.float32)
    dots = floats * cosines
    query_dot = jnp.sum(dots[:pair_dev], axis=1, keepdims=True)
    pin_dot = jnp.sum(dots.T[:pair_dev], axis=1, keepdims=True)
    query_step = jnp.dot(weights[:pair_dev], own_pins, preferred_element_type=jnp.float32)
    pin_step = jnp.dot(
        floats.T[:pair_dev].astype(jnp.bfloat16),
        units[0][:pairs],
        preferred_element_type=jnp.float32,
    )
    columns = pl.ds(pl.multiple_of(section * width, 128), width)
    for ref, step, dot, grad, fresh_first in (
        (query_ref, query_step, query_dot, grad_query, False),
        (pin_ref, pin_step, pin_dot, grad_pin, True),
    ):
        whole = ref[...].astype(jnp.float32)
        length = jnp.sqrt(jnp.sum(whole * whole, axis=1, keepdims=True) + EPSILON)
        unit = ref[:, columns].astype(jnp.float32) / length
        if fresh_first:
            is_first = numbers((pair_dev, 1), 0) == 0
            length = jnp.where(is_first, fresh_length[:1], length)
            unit = jnp.where(is_first, own_unit, unit)
        grad[...] = (step - unit * dot) / length


def local(held, norm_gain, w_gate, w_up, w_down, layer_counts, query_bank, pin_bank, positive):
    replicas = lax.axis_size("dp")
    sections = lax.axis_size("section")
    rows_dev, model_width = held.shape[1:]
    pair_dev = query_bank.shape[0]
    half = replicas // 2
    cut = rows_dev // 2
    order = ring_order(replicas)
    ring = [(order[i], order[(i + 1) % replicas]) for i in range(replicas)]
    ring_back = [(b, a) for a, b in ring]
    me = lax.axis_index("dp")
    section = lax.axis_index("section")
    position = jnp.where(me % 2 == 0, me // 2, replicas - (me + 1) // 2)
    position = position.reshape(1)
    last = sections - 1
    active = layer_counts[0] > 0
    stream = held[0]
    col_width = model_width // sections
    col_start = (section * col_width).astype(jnp.uint32)
    position, col_start = lax.optimization_barrier((position, col_start))

    def forward(values):
        return lax.ppermute(values, "dp", ring)

    def backward(values):
        return lax.ppermute(values, "dp", ring_back)

    def own_columns(values):
        return lax.dynamic_slice(values, (jnp.uint32(0), col_start), (values.shape[0], col_width))

    def after(values, others):
        return lax.optimization_barrier((values, others))[0]

    def doubled(values, reach):
        other = lax.ppermute(values, "dp", [(i, i ^ reach) for i in range(replicas)])
        return jnp.concatenate([values, other], axis=1)

    def gathered(values, reach):
        while reach:
            values = doubled(values, reach)
            reach //= 2
        return values

    def added_up(values):
        reach = 1
        while reach < replicas:
            pairs = [(i * sections + last, (i ^ reach) * sections + last) for i in range(replicas)]
            values = values + lax.ppermute(values, BOTH, pairs)
            reach *= 2
        return values

    def unit_columns(query_bank, pin_bank):
        query_send = unit_rows(query_bank)[0].astype(jnp.bfloat16)
        pin_send = own_columns(unit_rows(pin_bank)[0].astype(jnp.bfloat16))
        numbers = jnp.pad(positive, (0, col_width - pair_dev)).astype(jnp.bfloat16)
        is_first = (jnp.arange(pair_dev) == 0)[:, None]
        return jnp.stack([own_columns(query_send), jnp.where(is_first, numbers, pin_send)])

    def gather_and_multiply():
        f_top, f_low = normalized(stream, norm_gain[0])
        b_top, b_low = f_top, f_low
        first = [f_top, f_low]
        f_top, b_low = forward(f_top), backward(b_low)
        count = positive.astype(jnp.float32)
        f_low, b_top = after((f_low, b_top), count)
        f_low, b_top = forward(f_low), backward(b_top)
        own, tails, weights = multiply(
            first, [w_gate[0, 0], w_up[0, 0], w_down[0, 0]], True
        )
        sends = unit_columns(*after((query_bank, pin_bank), own))
        reach = half
        ready_near, ready_far = own, own
        terms_f, terms_b, all_tails = [], [], [tails]
        for step in range(1, half):
            near, rest = (f_top, b_low), (f_low, b_top)
            f_top, b_low = after(near, ready_near)
            f_top, b_low = forward(f_top), backward(b_low)
            (tf_top, tb_low), near_tails = multiply(near, weights, False)
            ready_far = (tf_top, tb_low, ready_far)
            if step < half - 1:
                f_low, b_top = after(rest, ready_far)
                f_low, b_top = forward(f_low), backward(b_top)
            else:
                tf_send, tb_send = after((tf_top, tb_low), ready_far)
                f_low, b_top = forward(tb_send), backward(tf_send)
            if reach:
                sends = doubled(after(sends, near), reach)
                reach //= 2
            ready_far = sends
            (tf_low, tb_top), rest_tails = multiply(rest, weights, False)
            ready_near = (tf_low, tb_top)
            terms_f.append((tf_top, tf_low))
            terms_b.append((tb_top, tb_low))
            all_tails += [near_tails, rest_tails]
        sends = gathered(sends, reach)
        far, tails = multiply([f_top, b_low], weights, False)
        f_top, b_low = forward(far[0]), backward(far[1])
        (f_top, b_low), sends = lax.optimization_barrier(((f_top, b_low), sends))
        f_top, b_low = two_sums((terms_b[-1][0], f_top), (terms_f[-1][1], b_low))
        all_tails.append(tails)
        slots = (
            [(0, 1)]
            + [(2 * step - 1, 1) for step in range(1, half)]
            + [(2 * half - 1, 1)]
            + [(2 * step, 0) for step in range(half - 1, 0, -1)]
        )
        all_tails = after(all_tails, (f_top, b_low))
        f_top, b_low = forward(f_top), backward(b_low)
        rows = ring_rows(slots, all_tails, position, stream)
        fresh = added_up(rows).astype(jnp.bfloat16)
        moving = (f_top, f_low, b_top, b_low)
        return tuple(own), tuple(terms_f), tuple(terms_b), moving, fresh, sends

    def gather_only():
        fresh = added_up(
            ring_rows([(0, 0)] * replicas, [jnp.zeros((8, model_width), jnp.float32)], position, stream)
        )
        empty = jnp.zeros((cut, model_width), jnp.bfloat16)
        some = tuple((empty, empty) for _ in range(1, half))
        return (
            (empty, empty),
            some,
            some,
            (empty,) * 4,
            fresh.astype(jnp.bfloat16),
            gathered(unit_columns(query_bank, pin_bank), half),
        )

    own, terms_f, terms_b, moving, fresh, sends = lax.cond(
        active, gather_and_multiply, gather_only
    )

    pairs = sends.shape[1]
    fresh = jnp.where(section == last, fresh, jnp.zeros_like(fresh))
    fresh = fresh.reshape(replicas * sections, col_width)
    known = [jnp.concatenate([sends.reshape(2 * pairs, col_width), fresh])]
    offsets = [0]

    def section_swap(reach):
        offsets.extend([offset ^ reach for offset in offsets])
        swap = [(s, s ^ reach) for s in range(sections)]
        known.extend([lax.ppermute(message, "section", swap) for message in known])

    section_swap(sections // 2)

    def reduce_middle(moving):
        f_top, f_low, b_top, b_low = moving
        for distance in range(half - 2, 1, -1):
            to_f, to_b = terms_b[distance - 1], terms_f[distance - 1]
            f_low, b_top = two_sums((to_f[1], f_low), (to_b[0], b_top))
            f_low, b_top = forward(f_low), backward(b_top)
            f_top, b_low = two_sums((to_f[0], f_top), (to_b[1], b_low))
            f_top, b_low = forward(f_top), backward(b_low)
        return f_top, f_low, b_top, b_low

    moving = lax.cond(active, reduce_middle, lambda moving: moving, moving)
    known[1], moving = lax.optimization_barrier((known[1], moving))
    reach = sections // 4
    while reach:
        section_swap(reach)
        reach //= 2
    place_here = jnp.stack([me, section])

    def loss(known):
        grad = jax.ShapeDtypeStruct((pair_dev, col_width), jnp.float32)
        return pl.pallas_call(
            functools.partial(loss_kernel, offsets, replicas, pair_dev),
            out_shape=[grad, grad],
            in_specs=[pl.BlockSpec(memory_space=pltpu.SMEM)] + [IN_VMEM] * (len(known) + 2),
            out_specs=[IN_VMEM] * 2,
            compiler_params=pltpu.CompilerParams(vmem_limit_bytes=32 << 20),
        )(place_here, *known, query_bank, pin_bank)

    def reduce_last(moving, known):
        f_top, f_low, b_top, b_low = moving
        to_f, to_b = terms_b[0], terms_f[0]
        f_low, b_top = two_sums((to_f[1], f_low), (to_b[0], b_top))
        f_low, b_top = forward(f_low), backward(b_top)
        f_top, b_low = two_sums((to_f[0], f_top), (to_b[1], b_low))
        f_top, b_low = forward(f_top), backward(b_low)
        grads = loss(known)
        plan = (
            (((0, 0), (1, 0), (3, 0), (5, 0)), 0, 0),
            (((0, cut), (2, 0), (4, 0), (6, 0)), 0, cut),
        )
        sources = [stream, *own, f_top, f_low, b_top, b_low]
        return *sums(plan, sources, cut, [stream.shape], pltpu.HBM), *grads

    def keep_stream(moving, known):
        return stream + jnp.concatenate(own), *loss(known)

    stream_out, grad_query, grad_pin = lax.cond(active, reduce_last, keep_stream, moving, known)
    return (stream_out[None], grad_query, grad_pin)


def solution(mesh):
    return jax.shard_map(
        local,
        mesh=mesh,
        in_specs=(
            P("section", "dp", None),
            P("section", None, None),
            P("section", None, None, "dp"),
            P("section", None, None, "dp"),
            P("section", None, "dp", None),
            P("section"),
            P("dp", None),
            P("dp", None),
            P("dp"),
        ),
        out_specs=(P("section", "dp", None), P("dp", "section"), P("dp", "section")),
        check_vma=False,
    )
```
